128 devices in a mesh: dp: 16 (over z, x_hi, core), head: 8 (over y, x_lo).
Axes of the slice: x: 4 (x_hi: 2, x_lo: 2; x = x_hi * 2 + x_lo), y: 4, z: 4, core: 2. Of those that a mesh axis runs over, the one named last changes fastest.
Arguments:
- query_rows: bfloat16 [24576, 2048], P(('dp', 'head')), may hold values from -9 to 9
- key_rows: bfloat16 [24576, 2048], P(('dp', 'head')), may hold values from -9 to 9
- value_rows: bfloat16 [24576, 2048], P(('dp', 'head')), may hold values from -6 to 6
- out_grad: bfloat16 [24576, 3072], P(('dp', 'head')), may hold values from -24 to 24
- out_weight: bfloat16 [2048, 3072], P('head'), may hold values from -0.109375 to 0.109375
- clip_len: int32 [32], replicated, may hold values from 256 to 1024, as said below
- clip_group: int32 [32], replicated, may hold values from 0 to 15, as said below
- clip_start: int32 [32], replicated, may hold values from 0 to 1280, as said below
Outputs:
- grad_query: bfloat16 [24576, 2048], P(('dp', 'head'))
- grad_key: bfloat16 [24576, 2048], P(('dp', 'head'))
- grad_value: bfloat16 [24576, 2048], P(('dp', 'head'))
- grad_weight: float32 [2048, 3072], P('head', 'dp')
The draws below stay inside these ranges and needn't reach their ends.
Inputs may be any that keep to these rules, and one draw needn't show every extreme that they name: `clip_len`: clip 2 g starts in group g and stays there, with 6 to 8 units of 128 rows; clip 2 g + 1 has 2 to 4 units; some clip 2 g has 1024 rows and some clip 2 g + 1 has 512 rows. clip_group[2 g] = g and clip_group[2 g + 1] = (g + r) modulo the number of data groups, with one r common to all groups, 1 <= r <= half the number of data groups. `clip_start`: the two clips of a group lie in index order without intersection inside its 1536 rows, each start a multiple of 128.
All inputs are finite; a program needn't handle non-finite values.
Results may differ from the reference program's by a relative error of at most 0.029.
Values may be sent and summed in bfloat16 or wider, within the bound.
No kernel may reach another device: no remote copies, remote signals or barrier semaphores. Data moves between devices by JAX's collectives and lax.ppermute only.
A program may use at most 128 MiB of HBM per device.

```python
import jax
import jax.numpy as jnp
from jax import lax

D = 3072
HEAD_DIM = 128
HEADS = 16
QW = 2048
GRP_TOK = 1536
TOKENS = 24576
UNIT = 128
CLIP_MAX = 1024
MOVE_MAX = 512
N_DP = 16


def clip_layout(key):
    base = jax.random.fold_in(key, 202)
    keys_all = jax.random.split(base, 6)
    group_ids = jnp.arange(N_DP, dtype=jnp.int32)
    home_units = jax.random.randint(keys_all[0], (N_DP,), 6, 9)
    move_units = jax.random.randint(keys_all[1], (N_DP,), 2, 5)
    picked = jax.random.randint(keys_all[2], (2,), 0, N_DP)
    home_units = jnp.where(group_ids == picked[0], 8, home_units)
    move_units = jnp.where(group_ids == picked[1], 4, move_units)
    slack = 12 - home_units - move_units
    first_gap = jax.random.randint(keys_all[3], (N_DP,), 0, slack + 1)
    second_gap = jax.random.randint(keys_all[4], (N_DP,), 0, slack - first_gap + 1)
    shift_amount = jax.random.randint(keys_all[5], (), 1, N_DP // 2 + 1)
    lengths = jnp.stack([home_units, move_units], axis=1) * UNIT
    starts = jnp.stack([first_gap, first_gap + home_units + second_gap], axis=1) * UNIT
    groups = jnp.stack([group_ids, (group_ids + shift_amount) % N_DP], axis=1)
    return (lengths.reshape(-1).astype(jnp.int32), groups.reshape(-1).astype(jnp.int32), starts.reshape(-1).astype(jnp.int32))


def draw_query_rows(key, part):
    key = jax.random.fold_in(key, 1)
    rows_drawn = jax.random.truncated_normal(key, -4.0, 4.0, (TOKENS, QW))
    return rows_drawn.astype(jnp.bfloat16)


def draw_key_rows(key, part):
    key = jax.random.fold_in(key, 2)
    rows_drawn = jax.random.truncated_normal(key, -4.0, 4.0, (TOKENS, QW))
    return rows_drawn.astype(jnp.bfloat16)


def draw_clip_len(key, part):
    return clip_layout(key)[0]


def draw_clip_group(key, part):
    return clip_layout(key)[1]


def draw_clip_start(key, part):
    return clip_layout(key)[2]


def with_spikes(result, stream_key, source, target, shards_of, factor):
    def block_of(axis_at):
        return (jnp.arange(result.shape[axis_at]) // (result.shape[axis_at] // shards_of)).reshape((-1,) + (1,) * (result.ndim - 1 - axis_at))

    first = jax.random.permutation(stream_key, shards_of)[block_of(target)]
    second = (block_of(target) + shards_of // 2) % shards_of
    return jnp.where((block_of(source) == first) | (block_of(source) == second), factor * result, result)


def block_levels(own_key, extent, shards, low, high):
    gain, own = 1.0, jax.random.fold_in(own_key, 6)
    for dim, shards_of in shards:
        steps = jnp.exp(jax.random.uniform(jax.random.fold_in(own, dim), (shards_of,), jnp.float32, low / len(shards), high / len(shards)))
        gain = gain * jnp.repeat(steps, extent[dim] // shards_of).reshape([-1 if axis == dim else 1 for axis in range(len(extent))])
    return gain


def noise(stream_key, extent, width, bound, shards=(), kind=jnp.bfloat16):
    level = block_levels(stream_key, extent, shards, -0.22, 0.18) if shards else 1.0
    values = jax.random.normal(stream_key, extent, jnp.float32) * width * level
    return jnp.minimum(jnp.maximum(values, -bound), bound).astype(kind)


def bell_draw_with(key, shape, scale, bound, cuts, heavy, kind=jnp.bfloat16):
    array = scale * jax.random.normal(key, shape, jnp.float32)
    if cuts:
        array = array * block_levels(key, shape, cuts, -0.22, 0.18)
    return jnp.clip(with_spikes(array, jax.random.fold_in(key, 3), *heavy), -bound, bound).astype(kind)


def setup_inputs(seed: int = 0) -> dict:
    key_list = jax.random.split(jax.random.key(seed), 9)
    query_rows = draw_query_rows(jax.random.fold_in(key_list[8], 71), 0)
    key_rows = draw_key_rows(jax.random.fold_in(key_list[8], 71), 0)
    value_rows = noise(key_list[2], (TOKENS, QW), 1.0, 6.0, ((0, 128),))
    out_grad = bell_draw_with(key_list[3], (TOKENS, D), 1.0, 24.0, ((0, 128),), (0, 1, 128, 5.5))
    out_weight = noise(key_list[4], (QW, D), D ** -0.5, 0.109375, ((0, 8),))
    clip_len = draw_clip_len(jax.random.fold_in(key_list[8], 71), 0)
    clip_group = draw_clip_group(jax.random.fold_in(key_list[8], 71), 0)
    clip_start = draw_clip_start(jax.random.fold_in(key_list[8], 71), 0)
    return dict(query_rows=query_rows, key_rows=key_rows, value_rows=value_rows, out_grad=out_grad, out_weight=out_weight, clip_len=clip_len, clip_group=clip_group, clip_start=clip_start)


NEG_BIG = -1.0e30


def add_rows(running_sum, addition, first_row):
    current = lax.dynamic_slice_in_dim(running_sum, first_row, addition.shape[0], 0)
    return lax.dynamic_update_slice_in_dim(running_sum, current + addition, first_row, 0)


def reference(query_rows, key_rows, value_rows, out_grad, out_weight, clip_len, clip_group, clip_start):
    clip_count = clip_len.shape[0]
    clip_ids = jnp.arange(clip_count, dtype=jnp.int32)
    anchor = (clip_ids // 2).astype(jnp.int32)
    is_moving = (clip_ids % 2) == 1
    home_len = jnp.take(clip_len, (2 * clip_group).astype(jnp.int32))
    target_start = jnp.where(is_moving, home_len, 0).astype(jnp.int32)
    src_first = (anchor * GRP_TOK + clip_start).astype(jnp.int32)
    dst_first = (clip_group * GRP_TOK + target_start).astype(jnp.int32)
    att_scale = HEAD_DIM ** -0.5
    margin = jnp.zeros((CLIP_MAX, QW), jnp.bfloat16)
    padded_q = jnp.concatenate([query_rows, margin], axis=0)
    padded_k = jnp.concatenate([key_rows, margin], axis=0)
    padded_v = jnp.concatenate([value_rows, margin], axis=0)
    padded_dy = jnp.concatenate([out_grad, jnp.zeros((CLIP_MAX, D), jnp.bfloat16)], axis=0)
    w_heads = out_weight.astype(jnp.float32).reshape(HEADS, HEAD_DIM, D)

    def clip_pass(tile_rows):
        clip_shape = (tile_rows, HEADS, HEAD_DIM)
        positions = jnp.arange(tile_rows, dtype=jnp.int32)

        def one_clip(running, index):
            acc_q, acc_k, acc_v, acc_w = running
            src_row = src_first[index]
            dst_row = dst_first[index]
            in_clip = positions < clip_len[index]
            q_clip = lax.dynamic_slice_in_dim(padded_q, src_row, tile_rows, 0).astype(jnp.float32).reshape(clip_shape)
            k_clip = lax.dynamic_slice_in_dim(padded_k, src_row, tile_rows, 0).astype(jnp.float32).reshape(clip_shape)
            v_clip = lax.dynamic_slice_in_dim(padded_v, src_row, tile_rows, 0).astype(jnp.float32).reshape(clip_shape)
            dy_clip = lax.dynamic_slice_in_dim(padded_dy, dst_row, tile_rows, 0).astype(jnp.float32)
            same_clip = (in_clip[:, None] & in_clip[None, :]).astype(jnp.float32)
            scores = jnp.einsum("qhd,khd->hqk", q_clip, k_clip) * att_scale
            scores = jnp.where(same_clip[None] > 0.5, scores, NEG_BIG)
            row_peak = jnp.max(scores, axis=2, keepdims=True)
            unnorm = jnp.exp(scores - row_peak) * same_clip[None]
            row_total = jnp.sum(unnorm, axis=2, keepdims=True)
            row_total = jnp.where(in_clip[None, :, None], row_total, 1.0)
            attn_prob = unnorm / row_total
            prob_half = attn_prob.astype(jnp.bfloat16)
            attended = jnp.einsum("hqk,khd->qhd", prob_half.astype(jnp.float32), v_clip).astype(jnp.bfloat16)
            grad_att = jnp.einsum("qe,hde->qhd", dy_clip, w_heads).astype(jnp.bfloat16)
            grad_att_wide = grad_att.astype(jnp.float32)
            attended_wide = attended.astype(jnp.float32)
            grad_prob = jnp.einsum("qhd,khd->hqk", grad_att_wide, v_clip)
            row_dot = jnp.sum(grad_att_wide * attended_wide, axis=2)
            grad_score = (attn_prob * (grad_prob - jnp.transpose(row_dot)[:, :, None])).astype(jnp.bfloat16)
            score_wide = grad_score.astype(jnp.float32)
            grad_q = (jnp.einsum("hqk,khd->qhd", score_wide, k_clip) * att_scale).astype(jnp.bfloat16)
            grad_k = (jnp.einsum("hqk,qhd->khd", score_wide, q_clip) * att_scale).astype(jnp.bfloat16)
            grad_v = jnp.einsum("hqk,qhd->khd", prob_half.astype(jnp.float32), grad_att_wide).astype(jnp.bfloat16)
            acc_q = add_rows(acc_q, grad_q.reshape(tile_rows, QW), dst_row)
            acc_k = add_rows(acc_k, grad_k.reshape(tile_rows, QW), dst_row)
            acc_v = add_rows(acc_v, grad_v.reshape(tile_rows, QW), dst_row)
            acc_w = acc_w + jnp.einsum("qhd,qe->hde", attended_wide, dy_clip)
            return (acc_q, acc_k, acc_v, acc_w), None

        return one_clip

    empty_rows = jnp.zeros((TOKENS + CLIP_MAX, QW), jnp.bfloat16)
    empty_weight = jnp.zeros((HEADS, HEAD_DIM, D), jnp.float32)
    starting = (empty_rows, empty_rows, empty_rows, empty_weight)
    after_home, unused = lax.scan(clip_pass(CLIP_MAX), starting, clip_ids[0::2])
    finals, unused_too = lax.scan(clip_pass(MOVE_MAX), after_home, clip_ids[1::2])
    acc_q, acc_k, acc_v, acc_w = finals
    grad_weight = acc_w.reshape(QW, D) * (TOKENS ** -0.5)
    return acc_q[:TOKENS], acc_k[:TOKENS], acc_v[:TOKENS], grad_weight
```

```python
import functools

import jax
import jax.numpy as jnp
from jax import lax
from jax.experimental import pallas as pl
from jax.experimental.pallas import tpu as pltpu
from jax.sharding import PartitionSpec as P

D = 3072
HD = 128
FEAT = 256
ROWS = 192
GROUP = 1536
HOME = 1024
MOVE = 512
HOME_MIN = 768
MOVE_MIN = 256
QB = 256
SCALE = HD ** (-0.5)
EXP2_SCALE = SCALE * 1.4426950408889634
NEG_BIG = -1e30
NN = (((1,), (0,)), ((), ()))
NT = (((1,), (1,)), ((), ()))
VMEM = pl.BlockSpec(memory_space=pltpu.VMEM)
SMEM = pl.BlockSpec(memory_space=pltpu.SMEM)
PARAMS = pltpu.CompilerParams(vmem_limit_bytes=56 * 1024 * 1024)


def dot(a, b, dims=NN):
    return lax.dot_general(a, b, dims, preferred_element_type=jnp.float32)


def flip(x):
    return x.astype(jnp.float32).T.astype(x.dtype)


def shifted(x, axis, distance):
    n = lax.axis_size(axis)
    return lax.ppermute(x, axis, [((i - distance) % n, i) for i in range(n)])


def swapped(x):
    return lax.ppermute(x, "head", [(i, i ^ 1) for i in range(8)])


def forward_clip(read, length, rows, sure, prob_ref, att_ref, att_first):
    for head in range(2):
        k = read(1, head, 0, rows)
        v_t = flip(read(2, head, 0, rows))

        def block(step, _, head=head, k=k, v_t=v_t):
            first = pl.multiple_of(step * QB, QB)
            q = read(0, head, first, QB)
            scores = dot(k, q, NT)
            key = lax.broadcasted_iota(jnp.int32, (rows - sure, QB), 0) + sure
            scores = jnp.concatenate(
                [scores[:sure], jnp.where(key < length, scores[sure:], NEG_BIG)], axis=0
            )
            peak = jnp.max(scores, axis=0, keepdims=True)
            unnorm = jnp.exp2((scores - peak) * EXP2_SCALE)
            total = jnp.sum(unnorm, axis=0, keepdims=True)
            query = lax.broadcasted_iota(jnp.int32, (1, QB), 1) + first
            prob = (unnorm * jnp.where(query < length, 1.0 / total, 0.0)).astype(jnp.bfloat16)
            prob_ref[head, :, pl.ds(first, QB)] = prob
            att = dot(v_t, prob).T.astype(jnp.bfloat16)
            att_ref[pl.ds(pl.multiple_of(att_first + first, 128), QB), pl.ds(head * HD, HD)] = att
            return 0

        lax.fori_loop(0, rows // QB, block, 0)


def forward_kernel(meta_ref, qkv_ref, move_ref, att_ref, home_prob_ref, move_prob_ref):
    home_first, home_len, arrive_len = meta_ref[0], meta_ref[1], meta_ref[2]

    def read_home(which, head, first, count):
        start = pl.multiple_of(home_first + first, 128)
        return qkv_ref[pl.ds(start, count), pl.ds(which * FEAT + head * HD, HD)]

    def read_move(which, head, first, count):
        return move_ref[pl.ds(first, count), pl.ds(which * FEAT + head * HD, HD)]

    att_ref[HOME:, :] = jnp.zeros((GROUP - HOME, FEAT), jnp.bfloat16)
    forward_clip(read_home, home_len, HOME, HOME_MIN, home_prob_ref, att_ref, 0)
    forward_clip(read_move, arrive_len, MOVE, MOVE_MIN, move_prob_ref, att_ref, home_len)


def forward(meta, qkv, moved):
    return pl.pallas_call(
        forward_kernel,
        out_shape=(
            jax.ShapeDtypeStruct((GROUP, FEAT), jnp.bfloat16),
            jax.ShapeDtypeStruct((2, HOME, HOME), jnp.bfloat16),
            jax.ShapeDtypeStruct((2, MOVE, MOVE), jnp.bfloat16),
        ),
        in_specs=[SMEM, VMEM, VMEM],
        out_specs=(VMEM, VMEM, VMEM),
        compiler_params=PARAMS,
        cost_estimate=pl.CostEstimate(
            flops=6_000_000_000, bytes_accessed=10_000_000, transcendentals=2_600_000
        ),
        name="forward",
    )(meta, qkv, moved)


def project_kernel(count, has_sum, owner_ref, weight_ref, att_ref, *refs):
    blocks = refs[:count]
    sum_ref = refs[count] if has_sum else None
    grad_att_ref, out_ref = refs[-2:]
    weight = weight_ref[...]
    att_t = []
    for i, block in enumerate(blocks):
        first = pl.multiple_of(owner_ref[i] * ROWS, ROWS)
        att_t.append(flip(att_ref[pl.ds(first, ROWS), :]))
        grad_att_ref[i] = dot(block[...], weight, NT).astype(jnp.bfloat16)
    for column in range(0, D, 256):
        part = sum_ref[:, column : column + 256] if has_sum else None
        for i, block in enumerate(blocks):
            add = dot(att_t[i], block[:, column : column + 256])
            part = add if part is None else part + add
        out_ref[:, column : column + 256] = part.astype(out_ref.dtype)


def project(owners, weight, att, blocks, running, out_type):
    count = len(blocks)
    extra = [] if running is None else [running]
    return pl.pallas_call(
        functools.partial(project_kernel, count, running is not None),
        out_shape=(
            jax.ShapeDtypeStruct((count, ROWS, FEAT), jnp.bfloat16),
            jax.ShapeDtypeStruct((FEAT, D), out_type),
        ),
        in_specs=[SMEM] + [VMEM] * (2 + count + len(extra)),
        out_specs=(VMEM, VMEM),
        compiler_params=PARAMS,
        cost_estimate=pl.CostEstimate(
            flops=count * 600_000_000, bytes_accessed=count * 1_200_000, transcendentals=0
        ),
        name="project",
    )(owners, weight, att, *blocks, *extra)


def backward_clip(read, rows, prob_ref, row_first, ga_ref, att_ref, out_ref, key_acc, value_acc):
    for head in range(2):
        columns = pl.ds(head * HD, HD)
        k_t = flip(read(1, head, 0, rows))
        v = read(2, head, 0, rows)
        key_acc[:rows, :] = jnp.zeros((rows, HD), jnp.float32)
        value_acc[:rows, :] = jnp.zeros((rows, HD), jnp.float32)

        def block(step, _, head=head, columns=columns, k_t=k_t, v=v):
            first = pl.multiple_of(step * QB, QB)
            there = pl.ds(pl.multiple_of(row_first + first, 128), QB)
            q = read(0, head, first, QB)
            prob = prob_ref[head, :, pl.ds(first, QB)]
            grad_att = ga_ref[there, columns]
            product = grad_att.astype(jnp.float32) * att_ref[there, columns].astype(jnp.float32)
            row_dot = jnp.sum(product.T, axis=0, keepdims=True)
            grad_prob = dot(v, grad_att, NT)
            grad_score = (prob.astype(jnp.float32) * (grad_prob - row_dot)).astype(jnp.bfloat16)
            value_acc[:rows, :] += dot(prob, grad_att)
            key_acc[:rows, :] += dot(grad_score, q)
            grad_query = (dot(k_t, grad_score) * SCALE).T.astype(jnp.bfloat16)
            out_ref[there, columns] = grad_query
            return 0

        lax.fori_loop(0, rows // QB, block, 0)
        whole = pl.ds(pl.multiple_of(row_first, 128), rows)
        out_ref[whole, pl.ds(FEAT + head * HD, HD)] = (key_acc[:rows, :] * SCALE).astype(jnp.bfloat16)
        out_ref[whole, pl.ds(2 * FEAT + head * HD, HD)] = value_acc[:rows, :].astype(jnp.bfloat16)


def backward_kernel(
    meta_ref, qkv_ref, move_ref, att_ref, home_prob_ref, move_prob_ref, near_ref, far_ref,
    out_ref, ga_ref, key_acc, value_acc,
):
    home_first, home_len = meta_ref[0], meta_ref[1]
    for i in range(8):
        first = pl.multiple_of(meta_ref[4 + i] * ROWS, ROWS)
        ga_ref[pl.ds(first, ROWS), :] = near_ref[i] if i < 4 else far_ref[i - 4]

    def read_home(which, head, first, count):
        start = pl.multiple_of(home_first + first, 128)
        return qkv_ref[pl.ds(start, count), pl.ds(which * FEAT + head * HD, HD)]

    def read_move(which, head, first, count):
        return move_ref[pl.ds(first, count), pl.ds(which * FEAT + head * HD, HD)]

    out_ref[HOME:, :] = jnp.zeros((GROUP - HOME, 3 * FEAT), jnp.bfloat16)
    backward_clip(
        read_home, HOME, home_prob_ref, 0, ga_ref, att_ref, out_ref, key_acc, value_acc
    )
    backward_clip(
        read_move, MOVE, move_prob_ref, home_len, ga_ref, att_ref, out_ref, key_acc, value_acc
    )


def backward(meta, qkv, moved, att, home_prob, move_prob, near, far):
    return pl.pallas_call(
        backward_kernel,
        out_shape=jax.ShapeDtypeStruct((GROUP, 3 * FEAT), jnp.bfloat16),
        in_specs=[SMEM] + [VMEM] * 7,
        out_specs=VMEM,
        scratch_shapes=[
            pltpu.VMEM((GROUP, FEAT), jnp.bfloat16),
            pltpu.VMEM((HOME, HD), jnp.float32),
            pltpu.VMEM((HOME, HD), jnp.float32),
        ],
        compiler_params=PARAMS,
        cost_estimate=pl.CostEstimate(
            flops=10_000_000_000, bytes_accessed=12_000_000, transcendentals=0
        ),
        name="backward",
    )(meta, qkv, moved, att, home_prob, move_prob, near, far)


def local(query_rows, key_rows, value_rows, out_grad, out_weight, clip_len, clip_group, clip_start):
    groups = lax.axis_size("dp")
    group_id = lax.axis_index("dp")
    me = lax.axis_index("head")
    rotate_by = jnp.mod(clip_group[1] - clip_group[0], groups)
    source_group = jnp.mod(group_id - rotate_by, groups)
    send_first = clip_start[2 * group_id + 1]
    owners = jnp.stack(
        [
            me,
            me ^ 1,
            (me + 6) % 8,
            (me + 2) % 8,
            (me + 4) % 8,
            ((me + 2) % 8) ^ 1,
            ((me + 6) % 8) ^ 1,
            ((me + 4) % 8) ^ 1,
        ]
    ).astype(jnp.int32)
    meta = jnp.concatenate(
        [
            jnp.stack(
                [
                    clip_start[2 * group_id],
                    clip_len[2 * group_id],
                    clip_len[2 * source_group + 1],
                    jnp.int32(0),
                ]
            ),
            owners,
        ]
    ).astype(jnp.int32)

    dy_x = swapped(out_grad)
    dy_up = shifted(out_grad, "head", 2)
    dy_down = shifted(out_grad, "head", -2)

    packed = jnp.concatenate(
        [x.reshape(ROWS, 8, FEAT) for x in (query_rows, key_rows, value_rows)], axis=2
    )
    qkv = lax.all_to_all(packed, "head", split_axis=1, concat_axis=0, tiled=False)
    qkv = qkv.reshape(GROUP, 3 * FEAT)

    padded = jnp.concatenate([qkv, jnp.zeros((MOVE // 2, 3 * FEAT), jnp.bfloat16)], axis=0)
    outgoing = lax.dynamic_slice_in_dim(padded, send_first, MOVE, 0)

    half, third = ROWS // 2, ROWS // 3
    got_up = shifted(jnp.concatenate([dy_up[:half], dy_x[:half]]), "head", 2)
    got_down = shifted(jnp.concatenate([dy_down[half:], dy_x[:half]]), "head", -2)
    got_x = swapped(jnp.concatenate([dy_down[half:], dy_up[half:]]))
    far_a = jnp.concatenate([got_up[:half], got_down[:half]])
    far_b = jnp.concatenate([got_down[half:], got_x[:half]])
    far_c = jnp.concatenate([got_up[half:], got_x[half:]])
    far_d = jnp.concatenate(
        [
            shifted(far_c[:third], "head", 2),
            shifted(far_b[third : 2 * third], "head", -2),
            swapped(far_a[2 * third :]),
        ]
    )

    moved = lax.switch(
        rotate_by - 1,
        [functools.partial(shifted, axis="dp", distance=d) for d in range(1, groups // 2 + 1)],
        outgoing,
    )
    att, home_prob, move_prob = forward(meta, qkv, moved)
    near, part = project(
        owners[:4], out_weight, att, [out_grad, dy_x, dy_up, dy_down], None, jnp.float32
    )
    far, part = project(
        owners[4:], out_weight, att, [far_a, far_b, far_c, far_d], part, jnp.bfloat16
    )
    pieces = lax.all_to_all(
        part.reshape(FEAT, groups, D // groups), "dp", split_axis=1, concat_axis=0, tiled=False
    )
    grad_weight = jnp.sum(pieces.astype(jnp.float32), axis=0) * ((GROUP * groups) ** (-0.5))

    grads = backward(meta, qkv, moved, att, home_prob, move_prob, near, far)
    back = lax.all_to_all(
        grads.reshape(8, ROWS, 3 * FEAT), "head", split_axis=0, concat_axis=1, tiled=False
    )
    outs = [
        back[:, :, i * FEAT : (i + 1) * FEAT].reshape(ROWS, 8 * FEAT) for i in range(3)
    ]
    return (*outs, grad_weight)


def solution(mesh):
    rows = P(("dp", "head"), None)
    in_specs = (rows, rows, rows, rows, P("head", None), P(), P(), P())
    out_specs = (rows, rows, rows, P("head", "dp"))
    return jax.shard_map(local, mesh=mesh, in_specs=in_specs, out_specs=out_specs, check_vma=False)
```

```python
import functools

import jax
import jax.numpy as jnp
from jax import lax
from jax.experimental import pallas as pl
from jax.experimental.pallas import tpu as pltpu
from jax.sharding import PartitionSpec as P

D = 3072
HD = 128
FEAT = 256
ROWS = 192
GROUP = 1536
HOME = 1024
MOVE = 512
HOME_MIN = 768
MOVE_MIN = 256
QB = 256
SCALE = HD ** (-0.5)
EXP2_SCALE = SCALE * 1.4426950408889634
NEG_BIG = -1e30
NN = (((1,), (0,)), ((), ()))
NT = (((1,), (1,)), ((), ()))
VMEM = pl.BlockSpec(memory_space=pltpu.VMEM)
SMEM = pl.BlockSpec(memory_space=pltpu.SMEM)
PARAMS = pltpu.CompilerParams(vmem_limit_bytes=56 * 1024 * 1024)


def dot(a, b, dims=NN):
    return lax.dot_general(a, b, dims, preferred_element_type=jnp.float32)


def flip(x):
    return x.astype(jnp.float32).T.astype(x.dtype)


def shifted(x, axis, distance):
    n = lax.axis_size(axis)
    return lax.ppermute(x, axis, [((i - distance) % n, i) for i in range(n)])


def swapped(x):
    return lax.ppermute(x, "head", [(i, i ^ 1) for i in range(8)])


def forward_clip(read, length, rows, sure, prob_ref, att_ref, att_first):
    for head in range(2):
        k = read(1, head, 0, rows)
        v_t = flip(read(2, head, 0, rows))

        def block(step, _, head=head, k=k, v_t=v_t):
            first = pl.multiple_of(step * QB, QB)
            q = read(0, head, first, QB)
            scores = dot(k, q, NT)
            key = lax.broadcasted_iota(jnp.int32, (rows - sure, QB), 0) + sure
            scores = jnp.concatenate(
                [scores[:sure], jnp.where(key < length, scores[sure:], NEG_BIG)], axis=0
            )
            peak = jnp.max(scores, axis=0, keepdims=True)
            unnorm = jnp.exp2((scores - peak) * EXP2_SCALE)
            total = jnp.sum(unnorm, axis=0, keepdims=True)
            query = lax.broadcasted_iota(jnp.int32, (1, QB), 1) + first
            prob = (unnorm * jnp.where(query < length, 1.0 / total, 0.0)).astype(jnp.bfloat16)
            prob_ref[head, :, pl.ds(first, QB)] = prob
            att = dot(v_t, prob).T.astype(jnp.bfloat16)
            att_ref[pl.ds(pl.multiple_of(att_first + first, 128), QB), pl.ds(head * HD, HD)] = att
            return 0

        lax.fori_loop(0, rows // QB, block, 0)


def forward_home_kernel(meta_ref, qkv_ref, att_ref, prob_ref):
    home_first, home_len = meta_ref[0], meta_ref[1]

    def read(which, head, first, count):
        start = pl.multiple_of(home_first + first, 128)
        return qkv_ref[pl.ds(start, count), pl.ds(which * FEAT + head * HD, HD)]

    forward_clip(read, home_len, HOME, HOME_MIN, prob_ref, att_ref, 0)


def forward_home(meta, qkv):
    return pl.pallas_call(
        forward_home_kernel,
        out_shape=(
            jax.ShapeDtypeStruct((HOME, FEAT), jnp.bfloat16),
            jax.ShapeDtypeStruct((2, HOME, HOME), jnp.bfloat16),
        ),
        in_specs=[SMEM, VMEM],
        out_specs=(VMEM, VMEM),
        compiler_params=PARAMS,
        cost_estimate=pl.CostEstimate(
            flops=6_000_000_000, bytes_accessed=8_000_000, transcendentals=2_100_000
        ),
        name="forward_home",
    )(meta, qkv)


def forward_move_kernel(meta_ref, move_ref, home_att_ref, att_ref, prob_ref):
    home_len, arrive_len = meta_ref[1], meta_ref[2]

    def read(which, head, first, count):
        return move_ref[pl.ds(first, count), pl.ds(which * FEAT + head * HD, HD)]

    att_ref[:HOME, :] = home_att_ref[...]
    att_ref[HOME:, :] = jnp.zeros((GROUP - HOME, FEAT), jnp.bfloat16)
    forward_clip(read, arrive_len, MOVE, MOVE_MIN, prob_ref, att_ref, home_len)


def forward_move(meta, moved, home_att):
    return pl.pallas_call(
        forward_move_kernel,
        out_shape=(
            jax.ShapeDtypeStruct((GROUP, FEAT), jnp.bfloat16),
            jax.ShapeDtypeStruct((2, MOVE, MOVE), jnp.bfloat16),
        ),
        in_specs=[SMEM, VMEM, VMEM],
        out_specs=(VMEM, VMEM),
        compiler_params=PARAMS,
        cost_estimate=pl.CostEstimate(
            flops=1_500_000_000, bytes_accessed=3_000_000, transcendentals=500_000
        ),
        name="forward_move",
    )(meta, moved, home_att)


def project_kernel(count, has_sum, owner_ref, weight_ref, att_ref, *refs):
    blocks = refs[:count]
    sum_ref = refs[count] if has_sum else None
    grad_att_ref, out_ref, att_t, acc = refs[-4:]
    step = pl.program_id(0)

    @pl.when(step == 0)
    def _():
        picked = [
            att_ref[pl.ds(pl.multiple_of(owner_ref[i] * ROWS, ROWS), ROWS), :]
            for i in range(count)
        ]
        att_t[...] = flip(jnp.concatenate(picked, axis=0))
        acc[...] = jnp.zeros_like(acc)

    dy = jnp.concatenate([block[...] for block in blocks], axis=0)
    acc[...] += dot(dy, weight_ref[...], NT)
    part = dot(att_t[...], dy)
    if has_sum:
        part = part + sum_ref[0]
    out_ref[0] = part.astype(out_ref.dtype)

    @pl.when(step == pl.num_programs(0) - 1)
    def _():
        grad_att_ref[...] = acc[...].astype(jnp.bfloat16)


def project(owners, weight, att, blocks, running, out_type):
    count = len(blocks)
    extra = [] if running is None else [running]
    wide = D // 4
    part_spec = pl.BlockSpec((1, FEAT, wide), lambda j: (j, 0, 0))
    return pl.pallas_call(
        functools.partial(project_kernel, count, running is not None),
        grid=(4,),
        out_shape=(
            jax.ShapeDtypeStruct((count * ROWS, FEAT), jnp.bfloat16),
            jax.ShapeDtypeStruct((4, FEAT, wide), out_type),
        ),
        in_specs=[
            SMEM,
            pl.BlockSpec((FEAT, wide), lambda j: (0, j)),
            pl.BlockSpec((GROUP, FEAT), lambda j: (0, 0)),
            *[pl.BlockSpec((ROWS, wide), lambda j: (0, j))] * count,
            *[part_spec] * len(extra),
        ],
        out_specs=(pl.BlockSpec((count * ROWS, FEAT), lambda j: (0, 0)), part_spec),
        scratch_shapes=[
            pltpu.VMEM((FEAT, count * ROWS), jnp.bfloat16),
            pltpu.VMEM((count * ROWS, FEAT), jnp.float32),
        ],
        compiler_params=PARAMS,
        cost_estimate=pl.CostEstimate(
            flops=count * 600_000_000, bytes_accessed=count * 1_200_000, transcendentals=0
        ),
        name="project",
    )(owners, weight, att, *blocks, *extra)


def backward_clip(read, rows, prob_ref, row_first, ga_ref, att_ref, out_ref, key_acc, value_acc):
    for head in range(2):
        columns = pl.ds(head * HD, HD)
        k_t = flip(read(1, head, 0, rows))
        v = read(2, head, 0, rows)
        key_acc[:rows, :] = jnp.zeros((rows, HD), jnp.float32)
        value_acc[:rows, :] = jnp.zeros((rows, HD), jnp.float32)

        def block(step, _, head=head, columns=columns, k_t=k_t, v=v):
            first = pl.multiple_of(step * QB, QB)
            there = pl.ds(pl.multiple_of(row_first + first, 128), QB)
            q = read(0, head, first, QB)
            prob = prob_ref[head, :, pl.ds(first, QB)]
            grad_att = ga_ref[there, columns]
            product = grad_att.astype(jnp.float32) * att_ref[there, columns].astype(jnp.float32)
            row_dot = jnp.sum(product.T, axis=0, keepdims=True)
            grad_prob = dot(v, grad_att, NT)
            grad_score = (prob.astype(jnp.float32) * (grad_prob - row_dot)).astype(jnp.bfloat16)
            value_acc[:rows, :] += dot(prob, grad_att)
            key_acc[:rows, :] += dot(grad_score, q)
            grad_query = (dot(k_t, grad_score) * SCALE).T.astype(jnp.bfloat16)
            out_ref[there, columns] = grad_query
            return 0

        lax.fori_loop(0, rows // QB, block, 0)
        whole = pl.ds(pl.multiple_of(row_first, 128), rows)
        out_ref[whole, pl.ds(FEAT + head * HD, HD)] = (key_acc[:rows, :] * SCALE).astype(jnp.bfloat16)
        out_ref[whole, pl.ds(2 * FEAT + head * HD, HD)] = value_acc[:rows, :].astype(jnp.bfloat16)


def backward_kernel(
    meta_ref, qkv_ref, move_ref, att_ref, home_prob_ref, move_prob_ref,
    near_ref, far_ref, last_ref, out_ref, ga_ref, key_acc, value_acc,
):
    home_first, home_len = meta_ref[0], meta_ref[1]
    for i in range(8):
        first = pl.multiple_of(meta_ref[4 + i] * ROWS, ROWS)
        part, at = (near_ref, i) if i < 4 else (far_ref, i - 4) if i < 7 else (last_ref, 0)
        ga_ref[pl.ds(first, ROWS), :] = part[at * ROWS : (at + 1) * ROWS, :]

    def read_home(which, head, first, count):
        start = pl.multiple_of(home_first + first, 128)
        return qkv_ref[pl.ds(start, count), pl.ds(which * FEAT + head * HD, HD)]

    def read_move(which, head, first, count):
        return move_ref[pl.ds(first, count), pl.ds(which * FEAT + head * HD, HD)]

    out_ref[HOME:, :] = jnp.zeros((GROUP - HOME, 3 * FEAT), jnp.bfloat16)
    backward_clip(
        read_home, HOME, home_prob_ref, 0, ga_ref, att_ref, out_ref, key_acc, value_acc
    )
    backward_clip(
        read_move, MOVE, move_prob_ref, home_len, ga_ref, att_ref, out_ref, key_acc, value_acc
    )


def backward(meta, qkv, moved, att, home_prob, move_prob, near, far, last):
    return pl.pallas_call(
        backward_kernel,
        out_shape=jax.ShapeDtypeStruct((GROUP, 3 * FEAT), jnp.bfloat16),
        in_specs=[SMEM] + [VMEM] * 8,
        out_specs=VMEM,
        scratch_shapes=[
            pltpu.VMEM((GROUP, FEAT), jnp.bfloat16),
            pltpu.VMEM((HOME, HD), jnp.float32),
            pltpu.VMEM((HOME, HD), jnp.float32),
        ],
        compiler_params=PARAMS,
        cost_estimate=pl.CostEstimate(
            flops=10_000_000_000, bytes_accessed=12_000_000, transcendentals=0
        ),
        name="backward",
    )(meta, qkv, moved, att, home_prob, move_prob, near, far, last)


def dp_swapped(x, mask):
    return lax.ppermute(x, "dp", [(i, i ^ mask) for i in range(16)])


def summed_over_dp(parts):
    group_id = lax.axis_index("dp")
    z, sub = group_id // 4, group_id % 4
    total = lax.dynamic_index_in_dim(parts, z, 0, keepdims=False).astype(jnp.float32)
    for distance in (1, 2, 3):
        sent = lax.dynamic_index_in_dim(parts, (z + distance) % 4, 0, keepdims=False)
        total = total + shifted(sent, "dp", 4 * distance).astype(jnp.float32)
    chunks = total.reshape(FEAT, 4, D // 16).transpose(1, 0, 2)
    mine = lax.dynamic_index_in_dim(chunks, sub, 0, keepdims=False)
    for mask in (1, 2, 3):
        sent = lax.dynamic_index_in_dim(chunks, sub ^ mask, 0, keepdims=False)
        mine = mine + dp_swapped(sent.astype(jnp.bfloat16), mask).astype(jnp.float32)
    return mine


def rotated(
    distance, query_rows, key_rows, value_rows, out_grad, out_weight, owners, meta, send_first
):
    dy_x = swapped(out_grad)
    dy_up = shifted(out_grad, "head", 2)
    dy_down = shifted(out_grad, "head", -2)

    packed = jnp.concatenate(
        [x.reshape(ROWS, 8, FEAT) for x in (query_rows, key_rows, value_rows)], axis=2
    )
    qkv = lax.all_to_all(packed, "head", split_axis=1, concat_axis=0, tiled=False)
    qkv = qkv.reshape(GROUP, 3 * FEAT)

    padded = jnp.concatenate([qkv, jnp.zeros((MOVE // 2, 3 * FEAT), jnp.bfloat16)], axis=0)
    outgoing = lax.dynamic_slice_in_dim(padded, send_first, MOVE, 0)
    moved = shifted(outgoing, "dp", distance)

    half, third = ROWS // 2, ROWS // 3
    got_up = shifted(jnp.concatenate([dy_up[:half], dy_x[:half]]), "head", 2)
    got_down = shifted(jnp.concatenate([dy_down[half:], dy_x[:half]]), "head", -2)
    got_x = swapped(jnp.concatenate([dy_down[half:], dy_up[half:]]))
    far_a = jnp.concatenate([got_up[:half], got_down[:half]])
    far_b = jnp.concatenate([got_down[half:], got_x[:half]])
    far_c = jnp.concatenate([got_up[half:], got_x[half:]])
    far_d = jnp.concatenate(
        [
            shifted(got_up[half : half + third], "head", 2),
            shifted(far_b[third : 2 * third], "head", -2),
            swapped(got_down[half - third : half]),
        ]
    )

    home_att, home_prob = forward_home(meta, qkv)
    att, move_prob = forward_move(meta, moved, home_att)
    near, part = project(
        owners[:4], out_weight, att, [out_grad, dy_x, dy_up, dy_down], None, jnp.float32
    )
    far, part = project(owners[4:7], out_weight, att, [far_a, far_b, far_c], part, jnp.float32)
    last, part = project(owners[7:], out_weight, att, [far_d], part, jnp.bfloat16)
    grad_weight = summed_over_dp(part) * ((GROUP * 16) ** (-0.5))

    grads = backward(meta, qkv, moved, att, home_prob, move_prob, near, far, last)
    back = lax.all_to_all(
        grads.reshape(8, ROWS, 3 * FEAT), "head", split_axis=0, concat_axis=1, tiled=False
    )
    outs = [
        back[:, :, i * FEAT : (i + 1) * FEAT].reshape(ROWS, 8 * FEAT) for i in range(3)
    ]
    return (*outs, grad_weight)


def local(query_rows, key_rows, value_rows, out_grad, out_weight, clip_len, clip_group, clip_start):
    groups = lax.axis_size("dp")
    group_id = lax.axis_index("dp")
    me = lax.axis_index("head")
    rotate_by = jnp.mod(clip_group[1] - clip_group[0], groups)
    source_group = jnp.mod(group_id - rotate_by, groups)
    owners = jnp.stack(
        [
            me,
            me ^ 1,
            (me + 6) % 8,
            (me + 2) % 8,
            (me + 4) % 8,
            ((me + 2) % 8) ^ 1,
            ((me + 6) % 8) ^ 1,
            ((me + 4) % 8) ^ 1,
        ]
    ).astype(jnp.int32)
    meta = jnp.concatenate(
        [
            jnp.stack(
                [
                    clip_start[2 * group_id],
                    clip_len[2 * group_id],
                    clip_len[2 * source_group + 1],
                    jnp.int32(0),
                ]
            ),
            owners,
        ]
    ).astype(jnp.int32)
    return lax.switch(
        rotate_by - 1,
        [functools.partial(rotated, d) for d in range(1, groups // 2 + 1)],
        query_rows, key_rows, value_rows, out_grad, out_weight, owners, meta,
        clip_start[2 * group_id + 1],
    )


def solution(mesh):
    rows = P(("dp", "head"), None)
    in_specs = (rows, rows, rows, rows, P("head", None), P(), P(), P())
    out_specs = (rows, rows, rows, P("head", "dp"))
    return jax.shard_map(local, mesh=mesh, in_specs=in_specs, out_specs=out_specs, check_vma=False)
```

```python
import functools

import jax
import jax.numpy as jnp
from jax import lax
from jax.experimental import pallas as pl
from jax.experimental.pallas import tpu as pltpu
from jax.sharding import Mesh, PartitionSpec as P

D = 3072
HD = 128
FEAT = 256
ROWS = 192
GROUP = 1536
HOME = 1024
MOVE = 512
HOME_MIN = 768
MOVE_MIN = 256
QB = 256
SCALE = HD ** (-0.5)
EXP2_SCALE = SCALE * 1.4426950408889634
NEG_BIG = -1e30
NN = (((1,), (0,)), ((), ()))
NT = (((1,), (1,)), ((), ()))
VMEM = pl.BlockSpec(memory_space=pltpu.VMEM)
SMEM = pl.BlockSpec(memory_space=pltpu.SMEM)
PARAMS = pltpu.CompilerParams(vmem_limit_bytes=56 * 1024 * 1024)


def dot(a, b, dims=NN):
    return lax.dot_general(a, b, dims, preferred_element_type=jnp.float32)


def flip(x):
    return x.astype(jnp.float32).T.astype(x.dtype)


def along(x, axis, distance):
    n = lax.axis_size(axis)
    return lax.ppermute(x, axis, [(i, (i + distance) % n) for i in range(n)])


def swapped(x):
    return lax.ppermute(
        x, ("core", "xlo"), [(c * 2 + d, d * 2 + c) for c in range(2) for d in range(2)]
    )


def other_core(x):
    return lax.ppermute(x, "core", [(0, 1), (1, 0)])


def forward_clip(read, length, rows, sure, prob_ref, att_ref, att_first):
    for head in range(2):
        k = read(1, head, 0, rows)
        v_t = flip(read(2, head, 0, rows))

        def block(step, _, head=head, k=k, v_t=v_t):
            first = pl.multiple_of(step * QB, QB)
            q = read(0, head, first, QB)
            scores = dot(k, q, NT)
            key = lax.broadcasted_iota(jnp.int32, (rows - sure, QB), 0) + sure
            scores = jnp.concatenate(
                [scores[:sure], jnp.where(key < length, scores[sure:], NEG_BIG)], axis=0
            )
            peak = jnp.max(scores, axis=0, keepdims=True)
            unnorm = jnp.exp2((scores - peak) * EXP2_SCALE)
            total = jnp.sum(unnorm, axis=0, keepdims=True)
            query = lax.broadcasted_iota(jnp.int32, (1, QB), 1) + first
            prob = (unnorm * jnp.where(query < length, 1.0 / total, 0.0)).astype(jnp.bfloat16)
            prob_ref[head, :, pl.ds(first, QB)] = prob
            att = dot(v_t, prob).T.astype(jnp.bfloat16)
            att_ref[pl.ds(pl.multiple_of(att_first + first, 128), QB), pl.ds(head * HD, HD)] = att
            return 0

        lax.fori_loop(0, rows // QB, block, 0)


def forward_home_kernel(meta_ref, qkv_ref, att_ref, prob_ref):
    home_first, home_len = meta_ref[0], meta_ref[1]

    def read(which, head, first, count):
        start = pl.multiple_of(home_first + first, 128)
        return qkv_ref[pl.ds(start, count), pl.ds(which * FEAT + head * HD, HD)]

    forward_clip(read, home_len, HOME, HOME_MIN, prob_ref, att_ref, 0)


def forward_home(meta, qkv):
    return pl.pallas_call(
        forward_home_kernel,
        out_shape=(
            jax.ShapeDtypeStruct((HOME, FEAT), jnp.bfloat16),
            jax.ShapeDtypeStruct((2, HOME, HOME), jnp.bfloat16),
        ),
        in_specs=[SMEM, VMEM],
        out_specs=(VMEM, VMEM),
        compiler_params=PARAMS,
        cost_estimate=pl.CostEstimate(
            flops=6_000_000_000, bytes_accessed=8_000_000, transcendentals=2_100_000
        ),
        name="forward_home",
    )(meta, qkv)


def forward_move_kernel(meta_ref, move_ref, home_att_ref, att_ref, prob_ref):
    home_len, arrive_len = meta_ref[1], meta_ref[2]

    def read(which, head, first, count):
        return move_ref[pl.ds(first, count), pl.ds(which * FEAT + head * HD, HD)]

    att_ref[:HOME, :] = home_att_ref[...]
    att_ref[HOME:, :] = jnp.zeros((GROUP - HOME, FEAT), jnp.bfloat16)
    forward_clip(read, arrive_len, MOVE, MOVE_MIN, prob_ref, att_ref, home_len)


def forward_move(meta, moved, home_att):
    return pl.pallas_call(
        forward_move_kernel,
        out_shape=(
            jax.ShapeDtypeStruct((GROUP, FEAT), jnp.bfloat16),
            jax.ShapeDtypeStruct((2, MOVE, MOVE), jnp.bfloat16),
        ),
        in_specs=[SMEM, VMEM, VMEM],
        out_specs=(VMEM, VMEM),
        compiler_params=PARAMS,
        cost_estimate=pl.CostEstimate(
            flops=1_500_000_000, bytes_accessed=3_000_000, transcendentals=500_000
        ),
        name="forward_move",
    )(meta, moved, home_att)


def grad_att_kernel(count, weight_ref, *refs):
    blocks = refs[:count]
    out_ref, acc = refs[-2:]
    step = pl.program_id(0)

    @pl.when(step == 0)
    def _():
        acc[...] = jnp.zeros_like(acc)

    dy = jnp.concatenate([block[...] for block in blocks], axis=0)
    acc[...] += dot(dy, weight_ref[...], NT)

    @pl.when(step == pl.num_programs(0) - 1)
    def _():
        out_ref[...] = acc[...].astype(jnp.bfloat16)


def grad_att(weight, blocks):
    count = len(blocks)
    wide = D // 4
    return pl.pallas_call(
        functools.partial(grad_att_kernel, count),
        grid=(4,),
        out_shape=jax.ShapeDtypeStruct((count * ROWS, FEAT), jnp.bfloat16),
        in_specs=[
            pl.BlockSpec((FEAT, wide), lambda j: (0, j)),
            *[pl.BlockSpec((ROWS, wide), lambda j: (0, j))] * count,
        ],
        out_specs=pl.BlockSpec((count * ROWS, FEAT), lambda j: (0, 0)),
        scratch_shapes=[pltpu.VMEM((count * ROWS, FEAT), jnp.float32)],
        compiler_params=PARAMS,
        cost_estimate=pl.CostEstimate(
            flops=count * 500_000_000, bytes_accessed=count * 1_200_000, transcendentals=0
        ),
        name="grad_att",
    )(weight, *blocks)


def grad_weight_kernel(count, owner_ref, att_ref, *refs):
    blocks = refs[:count]
    out_ref, att_t = refs[-2:]

    @pl.when(pl.program_id(0) == 0)
    def _():
        picked = [
            att_ref[pl.ds(pl.multiple_of(owner_ref[i] * ROWS, ROWS), ROWS), :]
            for i in range(count)
        ]
        att_t[...] = flip(jnp.concatenate(picked, axis=0))

    dy = jnp.concatenate([block[...] for block in blocks], axis=0)
    out_ref[0] = dot(att_t[...], dy).astype(out_ref.dtype)


def grad_weight_parts(owners, att, blocks):
    count = len(blocks)
    wide = D // 4
    return pl.pallas_call(
        functools.partial(grad_weight_kernel, count),
        grid=(4,),
        out_shape=jax.ShapeDtypeStruct((4, FEAT, wide), jnp.bfloat16),
        in_specs=[
            SMEM,
            pl.BlockSpec((GROUP, FEAT), lambda j: (0, 0)),
            *[pl.BlockSpec((ROWS, wide), lambda j: (0, j))] * count,
        ],
        out_specs=pl.BlockSpec((1, FEAT, wide), lambda j: (j, 0, 0)),
        scratch_shapes=[pltpu.VMEM((FEAT, count * ROWS), jnp.bfloat16)],
        compiler_params=PARAMS,
        cost_estimate=pl.CostEstimate(
            flops=4_000_000_000, bytes_accessed=11_000_000, transcendentals=0
        ),
        name="grad_weight",
    )(owners, att, *blocks)


def backward_clip(read, rows, prob_ref, row_first, ga_ref, att_ref, out_ref, key_acc, value_acc):
    for head in range(2):
        columns = pl.ds(head * HD, HD)
        k_t = flip(read(1, head, 0, rows))
        v = read(2, head, 0, rows)
        key_acc[:rows, :] = jnp.zeros((rows, HD), jnp.float32)
        value_acc[:rows, :] = jnp.zeros((rows, HD), jnp.float32)

        def block(step, _, head=head, columns=columns, k_t=k_t, v=v):
            first = pl.multiple_of(step * QB, QB)
            there = pl.ds(pl.multiple_of(row_first + first, 128), QB)
            q = read(0, head, first, QB)
            prob = prob_ref[head, :, pl.ds(first, QB)]
            grad_att = ga_ref[there, columns]
            product = grad_att.astype(jnp.float32) * att_ref[there, columns].astype(jnp.float32)
            row_dot = jnp.sum(product.T, axis=0, keepdims=True)
            grad_prob = dot(v, grad_att, NT)
            grad_score = (prob.astype(jnp.float32) * (grad_prob - row_dot)).astype(jnp.bfloat16)
            value_acc[:rows, :] += dot(prob, grad_att)
            key_acc[:rows, :] += dot(grad_score, q)
            grad_query = (dot(k_t, grad_score) * SCALE).T.astype(jnp.bfloat16)
            out_ref[there, columns] = grad_query
            return 0

        lax.fori_loop(0, rows // QB, block, 0)
        whole = pl.ds(pl.multiple_of(row_first, 128), rows)
        out_ref[whole, pl.ds(FEAT + head * HD, HD)] = (key_acc[:rows, :] * SCALE).astype(jnp.bfloat16)
        out_ref[whole, pl.ds(2 * FEAT + head * HD, HD)] = value_acc[:rows, :].astype(jnp.bfloat16)


def backward_kernel(
    meta_ref, qkv_ref, move_ref, att_ref, home_prob_ref, move_prob_ref,
    near_ref, far_ref, out_ref, ga_ref, key_acc, value_acc,
):
    home_first, home_len = meta_ref[0], meta_ref[1]
    for i in range(8):
        first = pl.multiple_of(meta_ref[4 + i] * ROWS, ROWS)
        part, at = (near_ref, i) if i < 6 else (far_ref, i - 6)
        ga_ref[pl.ds(first, ROWS), :] = part[at * ROWS : (at + 1) * ROWS, :]

    def read_home(which, head, first, count):
        start = pl.multiple_of(home_first + first, 128)
        return qkv_ref[pl.ds(start, count), pl.ds(which * FEAT + head * HD, HD)]

    def read_move(which, head, first, count):
        return move_ref[pl.ds(first, count), pl.ds(which * FEAT + head * HD, HD)]

    out_ref[HOME:, :] = jnp.zeros((GROUP - HOME, 3 * FEAT), jnp.bfloat16)
    backward_clip(
        read_home, HOME, home_prob_ref, 0, ga_ref, att_ref, out_ref, key_acc, value_acc
    )
    backward_clip(
        read_move, MOVE, move_prob_ref, home_len, ga_ref, att_ref, out_ref, key_acc, value_acc
    )


def backward(meta, qkv, moved, att, home_prob, move_prob, near, far):
    return pl.pallas_call(
        backward_kernel,
        out_shape=jax.ShapeDtypeStruct((GROUP, 3 * FEAT), jnp.bfloat16),
        in_specs=[SMEM] + [VMEM] * 7,
        out_specs=VMEM,
        scratch_shapes=[
            pltpu.VMEM((GROUP, FEAT), jnp.bfloat16),
            pltpu.VMEM((HOME, HD), jnp.float32),
            pltpu.VMEM((HOME, HD), jnp.float32),
        ],
        compiler_params=PARAMS,
        cost_estimate=pl.CostEstimate(
            flops=10_000_000_000, bytes_accessed=12_000_000, transcendentals=0
        ),
        name="backward",
    )(meta, qkv, moved, att, home_prob, move_prob, near, far)


def summed_over_groups(parts):
    z, xh, xlo = lax.axis_index("z"), lax.axis_index("xh"), lax.axis_index("xlo")
    total = lax.dynamic_index_in_dim(parts, z, 0, keepdims=False).astype(jnp.float32)
    for distance in (1, 2, 3):
        sent = lax.dynamic_index_in_dim(parts, (z + distance) % 4, 0, keepdims=False)
        total = total + along(sent, "z", distance).astype(jnp.float32)
    chunks = total.astype(jnp.bfloat16).reshape(FEAT, 4, D // 16).transpose(1, 0, 2)
    mine = None
    for a in range(2):
        for b in range(2):
            column = (xh ^ a) * 2 + (xlo ^ b)
            sent = lax.dynamic_index_in_dim(chunks, column, 0, keepdims=False)
            pairs = [
                ((h * 2 + c) * 2 + x, ((h ^ a) * 2 + (x ^ b)) * 2 + c)
                for h in range(2)
                for c in range(2)
                for x in range(2)
            ]
            got = lax.ppermute(sent, ("xh", "core", "xlo"), pairs).astype(jnp.float32)
            mine = got if mine is None else mine + got
    return mine


def arriving(distance, outgoing, qkv, meta, weight, own, own_o, up, down):
    moved = along(outgoing, ("z", "xh", "core"), distance)
    half = ROWS // 2
    far = jnp.concatenate([along(up[:half], "y", 1), along(down[half:], "y", -1)])
    up_o, down_o, far_o = other_core(up), other_core(down), other_core(far)
    home_att, home_prob = forward_home(meta, qkv)
    near = swapped(grad_att(weight, [own, own_o, up, up_o, down, down_o]))
    return moved, home_att, home_prob, near, up_o, down_o, far, far_o


def local(query_rows, key_rows, value_rows, out_grad, out_weight, clip_len, clip_group, clip_start):
    groups = 16
    xlo, core, y = lax.axis_index("xlo"), lax.axis_index("core"), lax.axis_index("y")
    group_id = (lax.axis_index("z") * 2 + lax.axis_index("xh")) * 2 + core
    rotate_by = jnp.mod(clip_group[1] - clip_group[0], groups)
    source_group = jnp.mod(group_id - rotate_by, groups)
    send_first = clip_start[2 * group_id + 1]

    def owners(low):
        return [
            2 * ((y + step) % 4) + side for step in (0, 3, 1, 2) for side in (low, 1 - low)
        ]

    meta = jnp.stack(
        [
            clip_start[2 * group_id],
            clip_len[2 * group_id],
            clip_len[2 * source_group + 1],
            jnp.int32(0),
            *owners(xlo),
        ]
    ).astype(jnp.int32)
    project_owners = jnp.stack(owners(core)).astype(jnp.int32)

    own = swapped(out_grad)
    up, down = along(own, "y", 1), along(own, "y", -1)
    own_o = other_core(own)
    weight = swapped(out_weight)

    packed = jnp.concatenate(
        [x.reshape(ROWS, 8, FEAT) for x in (query_rows, key_rows, value_rows)], axis=2
    )
    qkv = lax.all_to_all(packed, ("y", "xlo"), split_axis=1, concat_axis=0, tiled=False)
    qkv = qkv.reshape(GROUP, 3 * FEAT)
    padded = jnp.concatenate([qkv, jnp.zeros((MOVE // 2, 3 * FEAT), jnp.bfloat16)], axis=0)
    outgoing = lax.dynamic_slice_in_dim(padded, send_first, MOVE, 0)

    moved, home_att, home_prob, near, up_o, down_o, far, far_o = lax.switch(
        rotate_by - 1,
        [functools.partial(arriving, d) for d in range(1, groups // 2 + 1)],
        outgoing, qkv, meta, weight, own, own_o, up, down,
    )
    last = swapped(grad_att(weight, [far, far_o]))
    att, move_prob = forward_move(meta, moved, home_att)
    parts = grad_weight_parts(
        project_owners, swapped(att), [own, own_o, up, up_o, down, down_o, far, far_o]
    )
    grad_weight = summed_over_groups(parts) * ((GROUP * groups) ** (-0.5))

    grads = backward(meta, qkv, moved, att, home_prob, move_prob, near, last)
    back = lax.all_to_all(
        grads.reshape(8, ROWS, 3 * FEAT), ("y", "xlo"), split_axis=0, concat_axis=1, tiled=False
    )
    outs = [
        back[:, :, i * FEAT : (i + 1) * FEAT].reshape(ROWS, 8 * FEAT) for i in range(3)
    ]
    return (*outs, grad_weight)


def solution(mesh):
    axes = ("z", "xh", "core", "y", "xlo")
    fine = Mesh(mesh.devices.reshape(4, 2, 2, 4, 2), axes)
    rows = P(axes, None)
    head = P(("y", "xlo"), None)
    in_specs = (rows, rows, rows, rows, head, P(), P(), P())
    out_specs = (rows, rows, rows, P(("y", "xlo"), ("z", "xh", "core")))
    return jax.shard_map(local, mesh=fine, in_specs=in_specs, out_specs=out_specs, check_vma=False)
```

```python
import functools

import jax
import jax.numpy as jnp
from jax import lax
from jax.experimental import pallas as pl
from jax.experimental.pallas import tpu as pltpu
from jax.sharding import PartitionSpec as P

D = 3072
HD = 128
FEAT = 256
ROWS = 192
GROUP = 1536
HOME = 1024
MOVE = 512
HOME_MIN = 768
MOVE_MIN = 256
QB = 256
SCALE = HD ** (-0.5)
EXP2_SCALE = SCALE * 1.4426950408889634
NEG_BIG = -1e30
NN = (((1,), (0,)), ((), ()))
NT = (((1,), (1,)), ((), ()))
VMEM = pl.BlockSpec(memory_space=pltpu.VMEM)
SMEM = pl.BlockSpec(memory_space=pltpu.SMEM)
PARAMS = pltpu.CompilerParams(vmem_limit_bytes=56 * 1024 * 1024)


def dot(a, b, dims=NN):
    return lax.dot_general(a, b, dims, preferred_element_type=jnp.float32)


def flip(x):
    return x.astype(jnp.float32).T.astype(x.dtype)


def shifted(x, axis, distance):
    n = lax.axis_size(axis)
    return lax.ppermute(x, axis, [((i - distance) % n, i) for i in range(n)])


def swapped(x):
    return lax.ppermute(x, "head", [(i, i ^ 1) for i in range(8)])


def columns(which, head):
    return pl.ds(pl.multiple_of(which * FEAT + head * HD, HD), HD)


def forward_clip(read, length, rows, sure, prob_ref, att_ref, att_first):
    def one_head(head, _):
        k = read(1, head, 0, rows)
        v_t = flip(read(2, head, 0, rows))

        def block(step, _):
            first = pl.multiple_of(step * QB, QB)
            q = read(0, head, first, QB)
            scores = dot(k, q, NT)
            key = lax.broadcasted_iota(jnp.int32, (rows - sure, QB), 0) + sure
            scores = jnp.concatenate(
                [scores[:sure], jnp.where(key < length, scores[sure:], NEG_BIG)], axis=0
            )
            peak = jnp.max(scores, axis=0, keepdims=True)
            unnorm = jnp.exp2((scores - peak) * EXP2_SCALE)
            total = jnp.sum(unnorm, axis=0, keepdims=True)
            query = lax.broadcasted_iota(jnp.int32, (1, QB), 1) + first
            prob = (unnorm * jnp.where(query < length, 1.0 / total, 0.0)).astype(jnp.bfloat16)
            prob_ref[head, :, pl.ds(first, QB)] = prob
            att = dot(v_t, prob).T.astype(jnp.bfloat16)
            there = pl.ds(pl.multiple_of(att_first + first, 128), QB)
            att_ref[there, columns(0, head)] = att
            return 0

        return lax.fori_loop(0, rows // QB, block, 0)

    lax.fori_loop(0, 2, one_head, 0)


def forward_home_kernel(meta_ref, qkv_ref, att_ref, prob_ref):
    home_first, home_len = meta_ref[0], meta_ref[1]

    def read(which, head, first, count):
        start = pl.multiple_of(home_first + first, 128)
        return qkv_ref[pl.ds(start, count), columns(which, head)]

    forward_clip(read, home_len, HOME, HOME_MIN, prob_ref, att_ref, 0)


def forward_home(meta, qkv):
    return pl.pallas_call(
        forward_home_kernel,
        out_shape=(
            jax.ShapeDtypeStruct((HOME, FEAT), jnp.bfloat16),
            jax.ShapeDtypeStruct((2, HOME, HOME), jnp.bfloat16),
        ),
        in_specs=[SMEM, VMEM],
        out_specs=(VMEM, VMEM),
        compiler_params=PARAMS,
        cost_estimate=pl.CostEstimate(
            flops=6_000_000_000, bytes_accessed=8_000_000, transcendentals=2_100_000
        ),
        name="forward_home",
    )(meta, qkv)


def forward_move_kernel(meta_ref, move_ref, home_att_ref, att_ref, prob_ref):
    home_len, arrive_len = meta_ref[1], meta_ref[2]

    def read(which, head, first, count):
        return move_ref[pl.ds(first, count), columns(which, head)]

    att_ref[:HOME, :] = home_att_ref[...]
    att_ref[HOME:, :] = jnp.zeros((GROUP - HOME, FEAT), jnp.bfloat16)
    forward_clip(read, arrive_len, MOVE, MOVE_MIN, prob_ref, att_ref, home_len)


def forward_move(meta, moved, home_att):
    return pl.pallas_call(
        forward_move_kernel,
        out_shape=(
            jax.ShapeDtypeStruct((GROUP, FEAT), jnp.bfloat16),
            jax.ShapeDtypeStruct((2, MOVE, MOVE), jnp.bfloat16),
        ),
        in_specs=[SMEM, VMEM, VMEM],
        out_specs=(VMEM, VMEM),
        compiler_params=PARAMS,
        cost_estimate=pl.CostEstimate(
            flops=1_500_000_000, bytes_accessed=3_000_000, transcendentals=500_000
        ),
        name="forward_move",
    )(meta, moved, home_att)


def grad_att_kernel(count, weight_ref, *refs):
    blocks = refs[:count]
    out_ref, acc = refs[-2:]
    step = pl.program_id(0)

    @pl.when(step == 0)
    def _():
        acc[...] = jnp.zeros_like(acc)

    dy = jnp.concatenate([block[...] for block in blocks], axis=0)
    acc[...] += dot(dy, weight_ref[...], NT)

    @pl.when(step == pl.num_programs(0) - 1)
    def _():
        out_ref[...] = acc[...].astype(jnp.bfloat16)


def grad_att(weight, blocks):
    count = len(blocks)
    total = sum(block.shape[0] for block in blocks)
    wide = D // 4
    return pl.pallas_call(
        functools.partial(grad_att_kernel, count),
        grid=(4,),
        out_shape=jax.ShapeDtypeStruct((total, FEAT), jnp.bfloat16),
        in_specs=[
            pl.BlockSpec((FEAT, wide), lambda j: (0, j)),
            *[pl.BlockSpec((block.shape[0], wide), lambda j: (0, j)) for block in blocks],
        ],
        out_specs=pl.BlockSpec((total, FEAT), lambda j: (0, 0)),
        scratch_shapes=[pltpu.VMEM((total, FEAT), jnp.float32)],
        compiler_params=PARAMS,
        cost_estimate=pl.CostEstimate(
            flops=total * 3_000_000, bytes_accessed=total * 6_500, transcendentals=0
        ),
        name="grad_att",
    )(weight, *blocks)


def place_rows(att_ref, first_ref, rows):
    picked, at = [], 0
    for count in rows:
        first = pl.multiple_of(first_ref[at], 32)
        picked.append(att_ref[pl.ds(first, count), :])
        at += 1
    return flip(jnp.concatenate(picked, axis=0))


def grad_weight_kernel(pieces, first_ref, att_ref, *refs):
    blocks = refs[:-2]
    out_ref, att_t = refs[-2:]

    @pl.when(pl.program_id(0) == 0)
    def _():
        att_t[...] = place_rows(att_ref, first_ref, pieces)

    dy = jnp.concatenate([block[...] for block in blocks], axis=0)
    out_ref[0] = dot(att_t[...], dy)


def grad_weight_part(firsts, att, blocks, pieces):
    total = sum(pieces)
    wide = D // 4
    return pl.pallas_call(
        functools.partial(grad_weight_kernel, pieces),
        grid=(4,),
        out_shape=jax.ShapeDtypeStruct((4, FEAT, wide), jnp.float32),
        in_specs=[
            SMEM,
            pl.BlockSpec((GROUP, FEAT), lambda j: (0, 0)),
            *[pl.BlockSpec((block.shape[0], wide), lambda j: (0, j)) for block in blocks],
        ],
        out_specs=pl.BlockSpec((1, FEAT, wide), lambda j: (j, 0, 0)),
        scratch_shapes=[pltpu.VMEM((FEAT, total), jnp.bfloat16)],
        compiler_params=PARAMS,
        cost_estimate=pl.CostEstimate(
            flops=total * 2_500_000, bytes_accessed=total * 8_000, transcendentals=0
        ),
        name="grad_weight",
    )(firsts, att, *blocks)


def grad_weight_last_kernel(first_ref, att_ref, *refs):
    blocks = refs[:3]
    sum_ref, out_ref, att_t = refs[3:]

    @pl.when(pl.program_id(0) == 0)
    def _():
        att_t[...] = place_rows(att_ref, first_ref, (ROWS,))

    dy = jnp.concatenate([block[...] for block in blocks], axis=0)
    part = sum_ref[0] + dot(att_t[...], dy)
    cut = D // 16
    for xh in range(2):
        for core in range(2):
            at = (2 * xh + core) * cut
            out_ref[core, 0, :, xh * cut : (xh + 1) * cut] = part[:, at : at + cut].astype(
                jnp.bfloat16
            )


def grad_weight_last(firsts, att, blocks, running):
    wide = D // 4
    return pl.pallas_call(
        grad_weight_last_kernel,
        grid=(4,),
        out_shape=jax.ShapeDtypeStruct((2, 4, FEAT, wide // 2), jnp.bfloat16),
        in_specs=[
            SMEM,
            pl.BlockSpec((GROUP, FEAT), lambda j: (0, 0)),
            *[pl.BlockSpec((block.shape[0], wide), lambda j: (0, j)) for block in blocks],
            pl.BlockSpec((1, FEAT, wide), lambda j: (j, 0, 0)),
        ],
        out_specs=pl.BlockSpec((2, 1, FEAT, wide // 2), lambda j: (0, j, 0, 0)),
        scratch_shapes=[pltpu.VMEM((FEAT, ROWS), jnp.bfloat16)],
        compiler_params=PARAMS,
        cost_estimate=pl.CostEstimate(
            flops=600_000_000, bytes_accessed=6_000_000, transcendentals=0
        ),
        name="grad_weight_last",
    )(firsts, att, *blocks, running)


def backward_clip(read, rows, prob_ref, row_first, ga_ref, att_ref, out_ref, key_acc, value_acc):
    def one_head(head, _):
        k_t = flip(read(1, head, 0, rows))
        v = read(2, head, 0, rows)
        key_acc[:rows, :] = jnp.zeros((rows, HD), jnp.float32)
        value_acc[:rows, :] = jnp.zeros((rows, HD), jnp.float32)

        def block(step, _):
            first = pl.multiple_of(step * QB, QB)
            there = pl.ds(pl.multiple_of(row_first + first, 128), QB)
            q = read(0, head, first, QB)
            prob = prob_ref[head, :, pl.ds(first, QB)]
            grad_att = ga_ref[there, columns(0, head)]
            attended = att_ref[there, columns(0, head)]
            product = grad_att.astype(jnp.float32) * attended.astype(jnp.float32)
            row_dot = jnp.sum(product.T, axis=0, keepdims=True)
            grad_prob = dot(v, grad_att, NT)
            grad_score = (prob.astype(jnp.float32) * (grad_prob - row_dot)).astype(jnp.bfloat16)
            value_acc[:rows, :] += dot(prob, grad_att)
            key_acc[:rows, :] += dot(grad_score, q)
            grad_query = (dot(k_t, grad_score) * SCALE).T.astype(jnp.bfloat16)
            out_ref[there, columns(0, head)] = grad_query
            return 0

        lax.fori_loop(0, rows // QB, block, 0)
        whole = pl.ds(pl.multiple_of(row_first, 128), rows)
        out_ref[whole, columns(1, head)] = (key_acc[:rows, :] * SCALE).astype(jnp.bfloat16)
        out_ref[whole, columns(2, head)] = value_acc[:rows, :].astype(jnp.bfloat16)
        return 0

    lax.fori_loop(0, 2, one_head, 0)


def backward_kernel(
    meta_ref, qkv_ref, move_ref, att_ref, home_prob_ref, move_prob_ref,
    near_ref, far_ref, last_ref, out_ref, ga_ref, key_acc, value_acc,
):
    home_first, home_len = meta_ref[0], meta_ref[1]
    half = ROWS // 2
    for i in range(4):
        first = pl.multiple_of(meta_ref[4 + i], half)
        ga_ref[pl.ds(first, ROWS), :] = near_ref[i * ROWS : (i + 1) * ROWS, :]
    for i in range(6):
        first = pl.multiple_of(meta_ref[8 + i], half)
        ga_ref[pl.ds(first, half), :] = far_ref[i * half : (i + 1) * half, :]
    ga_ref[pl.ds(pl.multiple_of(meta_ref[14], half), ROWS), :] = last_ref[...]

    def read_home(which, head, first, count):
        start = pl.multiple_of(home_first + first, 128)
        return qkv_ref[pl.ds(start, count), columns(which, head)]

    def read_move(which, head, first, count):
        return move_ref[pl.ds(first, count), columns(which, head)]

    out_ref[HOME:, :] = jnp.zeros((GROUP - HOME, 3 * FEAT), jnp.bfloat16)
    backward_clip(
        read_home, HOME, home_prob_ref, 0, ga_ref, att_ref, out_ref, key_acc, value_acc
    )
    backward_clip(
        read_move, MOVE, move_prob_ref, home_len, ga_ref, att_ref, out_ref, key_acc, value_acc
    )


def backward(meta, qkv, moved, att, home_prob, move_prob, near, far, last):
    return pl.pallas_call(
        backward_kernel,
        out_shape=jax.ShapeDtypeStruct((GROUP, 3 * FEAT), jnp.bfloat16),
        in_specs=[SMEM] + [VMEM] * 8,
        out_specs=VMEM,
        scratch_shapes=[
            pltpu.VMEM((GROUP, FEAT), jnp.bfloat16),
            pltpu.VMEM((HOME, HD), jnp.float32),
            pltpu.VMEM((HOME, HD), jnp.float32),
        ],
        compiler_params=PARAMS,
        cost_estimate=pl.CostEstimate(
            flops=10_000_000_000, bytes_accessed=12_000_000, transcendentals=0
        ),
        name="backward",
    )(meta, qkv, moved, att, home_prob, move_prob, near, far, last)


def pick(x, index):
    return lax.dynamic_index_in_dim(x, index, 0, keepdims=False)


def summed_over_groups(parts):
    group_id = lax.axis_index("dp")
    z, xh, core = group_id // 4, group_id // 2 % 2, group_id % 2
    got = lax.ppermute(pick(parts, 1 - core), "dp", [(i, i ^ 1) for i in range(16)])
    both = (pick(parts, core).astype(jnp.float32) + got.astype(jnp.float32)).astype(jnp.bfloat16)
    total = pick(both, z).astype(jnp.float32)
    for distance in (1, 2, 3):
        sent = pick(both, (z + distance) % 4)
        total = total + shifted(sent, "dp", 4 * distance).astype(jnp.float32)
    low, high = total[:, : D // 16], total[:, D // 16 :]
    sent = jnp.where(xh == 0, high, low).astype(jnp.bfloat16)
    got = lax.ppermute(sent, "dp", [(i, i ^ 2) for i in range(16)])
    return jnp.where(xh == 0, low, high) + got.astype(jnp.float32)


def arriving(distance, outgoing, qkv, meta):
    moved = shifted(outgoing, "dp", distance)
    home_att, home_prob = forward_home(meta, qkv)
    return moved, home_att, home_prob


def local(query_rows, key_rows, value_rows, out_grad, out_weight, clip_len, clip_group, clip_start):
    groups = lax.axis_size("dp")
    group_id = lax.axis_index("dp")
    me = lax.axis_index("head")
    rotate_by = jnp.mod(clip_group[1] - clip_group[0], groups)
    source_group = jnp.mod(group_id - rotate_by, groups)
    half, third = ROWS // 2, ROWS // 3

    up, down = ((me + 6) % 8) * ROWS, ((me + 2) % 8) * ROWS
    far_a = ((me + 4) % 8) * ROWS
    far_b, far_c = (((me + 2) % 8) ^ 1) * ROWS, (((me + 6) % 8) ^ 1) * ROWS
    far_d = (((me + 4) % 8) ^ 1) * ROWS
    meta = jnp.stack(
        [
            clip_start[2 * group_id],
            clip_len[2 * group_id],
            clip_len[2 * source_group + 1],
            jnp.int32(0),
            me * ROWS,
            (me ^ 1) * ROWS,
            up,
            down,
            far_a,
            far_c,
            far_a + half,
            far_b,
            far_b + half,
            far_c + half,
            far_d,
        ]
    ).astype(jnp.int32)

    dy_x = swapped(out_grad)
    dy_up = shifted(out_grad, "head", 2)
    dy_down = shifted(out_grad, "head", -2)

    packed = jnp.concatenate(
        [x.reshape(ROWS, 8, FEAT) for x in (query_rows, key_rows, value_rows)], axis=2
    )
    qkv = lax.all_to_all(packed, "head", split_axis=1, concat_axis=0, tiled=False)
    qkv = qkv.reshape(GROUP, 3 * FEAT)
    padded = jnp.concatenate([qkv, jnp.zeros((MOVE // 2, 3 * FEAT), jnp.bfloat16)], axis=0)
    outgoing = lax.dynamic_slice_in_dim(padded, clip_start[2 * group_id + 1], MOVE, 0)

    moved, home_att, home_prob = lax.switch(
        rotate_by - 1,
        [functools.partial(arriving, d) for d in range(1, groups // 2 + 1)],
        outgoing, qkv, meta,
    )

    moved, dy_x, dy_up, dy_down = lax.optimization_barrier((moved, dy_x, dy_up, dy_down))
    got_up = shifted(jnp.concatenate([dy_up[:half], dy_x[:half]]), "head", 2)
    got_down = shifted(jnp.concatenate([dy_down[half:], dy_x[:half]]), "head", -2)
    got_x = swapped(jnp.concatenate([dy_down[half:], dy_up[half:]]))
    att, move_prob = forward_move(meta, moved, home_att)
    near_blocks = [out_grad, dy_x, dy_up, dy_down]
    near = grad_att(out_weight, near_blocks)

    last_blocks = [
        shifted(got_up[half : half + third], "head", 2),
        swapped(jnp.concatenate([got_up[third:half], got_down[: 2 * third - half]])),
        shifted(got_x[half - third : half], "head", -2),
    ]
    far_blocks = [got_up, got_down, got_x]
    far = grad_att(out_weight, far_blocks)
    part = grad_weight_part(
        meta[4:14], att, near_blocks + far_blocks, (ROWS,) * 4 + (half,) * 6
    )
    last = grad_att(out_weight, last_blocks)
    grads = backward(meta, qkv, moved, att, home_prob, move_prob, near, far, last)
    parts = grad_weight_last(meta[14:], att, last_blocks, part)
    grad_weight = summed_over_groups(parts) * ((GROUP * groups) ** (-0.5))

    back = lax.all_to_all(
        grads.reshape(8, ROWS, 3 * FEAT), "head", split_axis=0, concat_axis=1, tiled=False
    )
    outs = [
        back[:, :, i * FEAT : (i + 1) * FEAT].reshape(ROWS, 8 * FEAT) for i in range(3)
    ]
    return (*outs, grad_weight)


def solution(mesh):
    rows = P(("dp", "head"), None)
    in_specs = (rows, rows, rows, rows, P("head", None), P(), P(), P())
    out_specs = (rows, rows, rows, P("head", "dp"))
    return jax.shard_map(local, mesh=mesh, in_specs=in_specs, out_specs=out_specs, check_vma=False)
```

```python
import functools

import jax
import jax.numpy as jnp
from jax import lax
from jax.experimental import pallas as pl
from jax.experimental.pallas import tpu as pltpu
from jax.sharding import PartitionSpec as P

D = 3072
HD = 128
FEAT = 256
ROWS = 192
GROUP = 1536
HOME = 1024
MOVE = 512
HOME_MIN = 768
MOVE_MIN = 256
QB = 256
SCALE = HD ** (-0.5)
EXP2_SCALE = SCALE * 1.4426950408889634
NEG_BIG = -1e30
NN = (((1,), (0,)), ((), ()))
NT = (((1,), (1,)), ((), ()))
VMEM = pl.BlockSpec(memory_space=pltpu.VMEM)
SMEM = pl.BlockSpec(memory_space=pltpu.SMEM)
PARAMS = pltpu.CompilerParams(vmem_limit_bytes=32 * 1024 * 1024)


def dot(a, b, dims=NN):
    return lax.dot_general(a, b, dims, preferred_element_type=jnp.float32)


def flip(x):
    return x.astype(jnp.float32).T.astype(x.dtype)


def apart_kernel(packed_ref, *outs):
    for i, out in enumerate(outs):
        out[...] = packed_ref[0, :, i * FEAT : (i + 1) * FEAT]


def apart(packed):
    return pl.pallas_call(
        apart_kernel,
        grid=(8,),
        out_shape=(jax.ShapeDtypeStruct((ROWS, 8 * FEAT), jnp.bfloat16),) * 3,
        in_specs=[pl.BlockSpec((1, ROWS, 3 * FEAT), lambda i: (i, 0, 0))],
        out_specs=(pl.BlockSpec((ROWS, FEAT), lambda i: (0, i)),) * 3,
        compiler_params=PARAMS,
        name="apart",
    )(packed)


def shifted(x, axis, distance):
    n = lax.axis_size(axis)
    return lax.ppermute(x, axis, [((i - distance) % n, i) for i in range(n)])


def swapped(x):
    return lax.ppermute(x, "head", [(i, i ^ 1) for i in range(8)])


def columns(which, head):
    return pl.ds(pl.multiple_of(which * FEAT + head * HD, HD), HD)


def forward_clip(read, length, rows, sure, prob_ref, att_ref, att_first):
    def one_head(head, _):
        k = read(1, head, 0, rows)
        v_t = flip(read(2, head, 0, rows))

        def block(step, _):
            first = pl.multiple_of(step * QB, QB)
            q = read(0, head, first, QB)
            scores = dot(k, q, NT)
            key = lax.broadcasted_iota(jnp.int32, (rows - sure, QB), 0) + sure
            scores = jnp.concatenate(
                [scores[:sure], jnp.where(key < length, scores[sure:], NEG_BIG)], axis=0
            )
            peak = jnp.max(scores, axis=0, keepdims=True)
            unnorm = jnp.exp2((scores - peak) * EXP2_SCALE)
            total = jnp.sum(unnorm, axis=0, keepdims=True)
            query = lax.broadcasted_iota(jnp.int32, (1, QB), 1) + first
            prob = (unnorm * jnp.where(query < length, 1.0 / total, 0.0)).astype(jnp.bfloat16)
            prob_ref[head, :, pl.ds(first, QB)] = prob
            att = dot(v_t, prob).T.astype(jnp.bfloat16)
            there = pl.ds(pl.multiple_of(att_first + first, 128), QB)
            att_ref[there, columns(0, head)] = att
            return 0

        return lax.fori_loop(0, rows // QB, block, 0)

    lax.fori_loop(0, 2, one_head, 0)


def forward_home_kernel(meta_ref, qkv_ref, att_ref, prob_ref):
    home_first, home_len = meta_ref[0], meta_ref[1]

    def read(which, head, first, count):
        start = pl.multiple_of(home_first + first, 128)
        return qkv_ref[pl.ds(start, count), columns(which, head)]

    forward_clip(read, home_len, HOME, HOME_MIN, prob_ref, att_ref, 0)


def forward_home(meta, qkv):
    return pl.pallas_call(
        forward_home_kernel,
        out_shape=(
            jax.ShapeDtypeStruct((HOME, FEAT), jnp.bfloat16),
            jax.ShapeDtypeStruct((2, HOME, HOME), jnp.bfloat16),
        ),
        in_specs=[SMEM, VMEM],
        out_specs=(VMEM, VMEM),
        compiler_params=PARAMS,
        cost_estimate=pl.CostEstimate(
            flops=6_000_000_000, bytes_accessed=8_000_000, transcendentals=2_100_000
        ),
        name="forward_home",
    )(meta, qkv)


def forward_move_kernel(meta_ref, move_ref, home_att_ref, att_ref, prob_ref):
    home_len, arrive_len = meta_ref[1], meta_ref[2]

    def read(which, head, first, count):
        return move_ref[pl.ds(first, count), columns(which, head)]

    att_ref[:HOME, :] = home_att_ref[...]
    att_ref[HOME:, :] = jnp.zeros((GROUP - HOME, FEAT), jnp.bfloat16)
    forward_clip(read, arrive_len, MOVE, MOVE_MIN, prob_ref, att_ref, home_len)


def forward_move(meta, moved, home_att):
    return pl.pallas_call(
        forward_move_kernel,
        out_shape=(
            jax.ShapeDtypeStruct((GROUP, FEAT), jnp.bfloat16),
            jax.ShapeDtypeStruct((2, MOVE, MOVE), jnp.bfloat16),
        ),
        in_specs=[SMEM, VMEM, VMEM],
        out_specs=(VMEM, VMEM),
        compiler_params=PARAMS,
        cost_estimate=pl.CostEstimate(
            flops=150_000_000, bytes_accessed=300_000, transcendentals=50_000
        ),
        name="forward_move",
    )(meta, moved, home_att)


def grad_att_kernel(count, weight_ref, *refs):
    blocks = refs[:count]
    out_ref, acc = refs[-2:]
    step = pl.program_id(0)

    @pl.when(step == 0)
    def _():
        acc[...] = jnp.zeros_like(acc)

    dy = jnp.concatenate([block[...] for block in blocks], axis=0)
    acc[...] += dot(dy, weight_ref[...], NT)

    @pl.when(step == pl.num_programs(0) - 1)
    def _():
        out_ref[...] = acc[...].astype(jnp.bfloat16)


def grad_att(weight, blocks):
    count = len(blocks)
    total = sum(block.shape[0] for block in blocks)
    wide = D // 4
    return pl.pallas_call(
        functools.partial(grad_att_kernel, count),
        grid=(4,),
        out_shape=jax.ShapeDtypeStruct((total, FEAT), jnp.bfloat16),
        in_specs=[
            pl.BlockSpec((FEAT, wide), lambda j: (0, j)),
            *[pl.BlockSpec((block.shape[0], wide), lambda j: (0, j)) for block in blocks],
        ],
        out_specs=pl.BlockSpec((total, FEAT), lambda j: (0, 0)),
        scratch_shapes=[pltpu.VMEM((total, FEAT), jnp.float32)],
        compiler_params=PARAMS,
        cost_estimate=pl.CostEstimate(
            flops=total * 300_000, bytes_accessed=total * 650, transcendentals=0
        ),
        name="grad_att",
    )(weight, *blocks)


def place_rows(att_ref, first_ref, rows):
    picked, at = [], 0
    for count in rows:
        first = pl.multiple_of(first_ref[at], 32)
        picked.append(att_ref[pl.ds(first, count), :])
        at += 1
    return flip(jnp.concatenate(picked, axis=0))


def grad_weight_kernel(pieces, first_ref, att_ref, *refs):
    blocks = refs[:-2]
    out_ref, att_t = refs[-2:]

    @pl.when(pl.program_id(0) == 0)
    def _():
        att_t[...] = place_rows(att_ref, first_ref, pieces)

    dy = jnp.concatenate([block[...] for block in blocks], axis=0)
    out_ref[0] = dot(att_t[...], dy)


def grad_weight_part(firsts, att, blocks, pieces):
    total = sum(pieces)
    wide = D // 4
    return pl.pallas_call(
        functools.partial(grad_weight_kernel, pieces),
        grid=(4,),
        out_shape=jax.ShapeDtypeStruct((4, FEAT, wide), jnp.float32),
        in_specs=[
            SMEM,
            pl.BlockSpec((GROUP, FEAT), lambda j: (0, 0)),
            *[pl.BlockSpec((block.shape[0], wide), lambda j: (0, j)) for block in blocks],
        ],
        out_specs=pl.BlockSpec((1, FEAT, wide), lambda j: (j, 0, 0)),
        scratch_shapes=[pltpu.VMEM((FEAT, total), jnp.bfloat16)],
        compiler_params=PARAMS,
        cost_estimate=pl.CostEstimate(
            flops=total * 250_000, bytes_accessed=total * 800, transcendentals=0
        ),
        name="grad_weight",
    )(firsts, att, *blocks)


def backward_clip(read, rows, prob_ref, row_first, ga_ref, att_ref, out_ref, key_acc, value_acc):
    def one_head(head, _):
        k_t = flip(read(1, head, 0, rows))
        v = read(2, head, 0, rows)
        key_acc[:rows, :] = jnp.zeros((rows, HD), jnp.float32)
        value_acc[:rows, :] = jnp.zeros((rows, HD), jnp.float32)

        def block(step, _):
            first = pl.multiple_of(step * QB, QB)
            there = pl.ds(pl.multiple_of(row_first + first, 128), QB)
            q = read(0, head, first, QB)
            prob = prob_ref[head, :, pl.ds(first, QB)]
            grad_att = ga_ref[there, columns(0, head)]
            attended = att_ref[there, columns(0, head)]
            product = grad_att.astype(jnp.float32) * attended.astype(jnp.float32)
            row_dot = jnp.sum(product.T, axis=0, keepdims=True)
            grad_prob = dot(v, grad_att, NT)
            grad_score = (prob.astype(jnp.float32) * (grad_prob - row_dot)).astype(jnp.bfloat16)
            value_acc[:rows, :] += dot(prob, grad_att)
            key_acc[:rows, :] += dot(grad_score, q)
            grad_query = (dot(k_t, grad_score) * SCALE).T.astype(jnp.bfloat16)
            out_ref[there, columns(0, head)] = grad_query
            return 0

        lax.fori_loop(0, rows // QB, block, 0)
        whole = pl.ds(pl.multiple_of(row_first, 128), rows)
        out_ref[whole, columns(1, head)] = (key_acc[:rows, :] * SCALE).astype(jnp.bfloat16)
        out_ref[whole, columns(2, head)] = value_acc[:rows, :].astype(jnp.bfloat16)
        return 0

    lax.fori_loop(0, 2, one_head, 0)


def backward_kernel(
    meta_ref, qkv_ref, move_ref, att_ref, home_prob_ref, move_prob_ref,
    near_ref, far_ref, weight_ref, last_a, last_b, last_c, sum_ref,
    out_ref, send_ref, keep_ref, ga_ref, key_acc, value_acc,
):
    home_first, home_len = meta_ref[0], meta_ref[1]
    half = ROWS // 2
    for i in range(4):
        first = pl.multiple_of(meta_ref[4 + i], half)
        ga_ref[pl.ds(first, ROWS), :] = near_ref[i * ROWS : (i + 1) * ROWS, :]
    for i in range(6):
        first = pl.multiple_of(meta_ref[8 + i], half)
        ga_ref[pl.ds(first, half), :] = far_ref[i * half : (i + 1) * half, :]
    dy = jnp.concatenate([last_a[...], last_b[...], last_c[...]], axis=0)
    last = dot(dy, weight_ref[...], NT).astype(jnp.bfloat16)
    last_rows = pl.ds(pl.multiple_of(meta_ref[14], half), ROWS)
    ga_ref[last_rows, :] = last

    att_t = flip(att_ref[last_rows, :])
    wide, cut = D // 4, D // 16
    for z in range(4):
        whole = sum_ref[z] + dot(att_t, dy[:, z * wide : (z + 1) * wide])
        by_core = [
            jnp.concatenate(
                [whole[:, (2 * xh + core) * cut : (2 * xh + core + 1) * cut] for xh in range(2)],
                axis=1,
            ).astype(jnp.bfloat16)
            for core in range(2)
        ]
        first_core = meta_ref[15] == 0
        keep_ref[z] = jnp.where(first_core, by_core[0], by_core[1])
        send_ref[z] = jnp.where(first_core, by_core[1], by_core[0])

    def read_home(which, head, first, count):
        start = pl.multiple_of(home_first + first, 128)
        return qkv_ref[pl.ds(start, count), columns(which, head)]

    def read_move(which, head, first, count):
        return move_ref[pl.ds(first, count), columns(which, head)]

    out_ref[HOME:, :] = jnp.zeros((GROUP - HOME, 3 * FEAT), jnp.bfloat16)
    backward_clip(
        read_home, HOME, home_prob_ref, 0, ga_ref, att_ref, out_ref, key_acc, value_acc
    )
    backward_clip(
        read_move, MOVE, move_prob_ref, home_len, ga_ref, att_ref, out_ref, key_acc, value_acc
    )


def backward(meta, qkv, moved, att, home_prob, move_prob, near, far, weight, last_blocks, part):
    return pl.pallas_call(
        backward_kernel,
        out_shape=(
            jax.ShapeDtypeStruct((GROUP, 3 * FEAT), jnp.bfloat16),
            jax.ShapeDtypeStruct((4, FEAT, D // 8), jnp.bfloat16),
            jax.ShapeDtypeStruct((4, FEAT, D // 8), jnp.bfloat16),
        ),
        in_specs=[SMEM] + [VMEM] * 12,
        out_specs=(VMEM, VMEM, VMEM),
        scratch_shapes=[
            pltpu.VMEM((GROUP, FEAT), jnp.bfloat16),
            pltpu.VMEM((HOME, HD), jnp.float32),
            pltpu.VMEM((HOME, HD), jnp.float32),
        ],
        compiler_params=PARAMS,
        cost_estimate=pl.CostEstimate(
            flops=10_000_000_000, bytes_accessed=12_000_000, transcendentals=0
        ),
        name="backward",
    )(meta, qkv, moved, att, home_prob, move_prob, near, far, weight, *last_blocks, part)


def pick(x, index):
    return lax.dynamic_index_in_dim(x, index, 0, keepdims=False)


def summed_over_groups(send, keep):
    group_id = lax.axis_index("dp")
    z, xh = group_id // 4, group_id // 2 % 2
    got = lax.ppermute(send, "dp", [(i, i ^ 1) for i in range(16)])
    both = (keep.astype(jnp.float32) + got.astype(jnp.float32)).astype(jnp.bfloat16)
    total = pick(both, z).astype(jnp.float32)
    for distance in (1, 2, 3):
        sent = pick(both, (z + distance) % 4)
        total = total + shifted(sent, "dp", 4 * distance).astype(jnp.float32)
    low, high = total[:, : D // 16], total[:, D // 16 :]
    sent = jnp.where(xh == 0, high, low).astype(jnp.bfloat16)
    got = lax.ppermute(sent, "dp", [(i, i ^ 2) for i in range(16)])
    return jnp.where(xh == 0, low, high) + got.astype(jnp.float32)


def arriving(distance, outgoing, qkv, meta, weight, *blocks):
    moved = shifted(outgoing, "dp", distance)
    home_att, home_prob = forward_home(meta, qkv)
    near = grad_att(weight, blocks)
    return moved, home_att, home_prob, near


def local(query_rows, key_rows, value_rows, out_grad, out_weight, clip_len, clip_group, clip_start):
    groups = lax.axis_size("dp")
    group_id = lax.axis_index("dp")
    me = lax.axis_index("head")
    rotate_by = jnp.mod(clip_group[1] - clip_group[0], groups)
    source_group = jnp.mod(group_id - rotate_by, groups)
    half, third = ROWS // 2, ROWS // 3

    up, down = ((me + 6) % 8) * ROWS, ((me + 2) % 8) * ROWS
    far_a = ((me + 4) % 8) * ROWS
    far_b, far_c = (((me + 2) % 8) ^ 1) * ROWS, (((me + 6) % 8) ^ 1) * ROWS
    far_d = (((me + 4) % 8) ^ 1) * ROWS
    meta = jnp.stack(
        [
            clip_start[2 * group_id],
            clip_len[2 * group_id],
            clip_len[2 * source_group + 1],
            jnp.int32(0),
            me * ROWS,
            (me ^ 1) * ROWS,
            up,
            down,
            far_a,
            far_c,
            far_a + half,
            far_b,
            far_b + half,
            far_c + half,
            far_d,
            group_id % 2,
        ]
    ).astype(jnp.int32)

    dy_x = swapped(out_grad)
    dy_up = shifted(out_grad, "head", 2)
    dy_down = shifted(out_grad, "head", -2)

    packed = jnp.concatenate(
        [x.reshape(ROWS, 8, FEAT) for x in (query_rows, key_rows, value_rows)], axis=2
    )
    qkv = lax.all_to_all(packed, "head", split_axis=1, concat_axis=0, tiled=False)
    qkv = qkv.reshape(GROUP, 3 * FEAT)
    padded = jnp.concatenate([qkv, jnp.zeros((MOVE // 2, 3 * FEAT), jnp.bfloat16)], axis=0)
    outgoing = lax.dynamic_slice_in_dim(padded, clip_start[2 * group_id + 1], MOVE, 0)

    got_up = shifted(jnp.concatenate([dy_up[:half], dy_x[:half]]), "head", 2)
    got_down = shifted(jnp.concatenate([dy_down[half:], dy_x[:half]]), "head", -2)
    got_x = swapped(jnp.concatenate([dy_down[half:], dy_up[half:]]))

    near_blocks = [out_grad, dy_x, dy_up, dy_down]
    moved, home_att, home_prob, near = lax.switch(
        rotate_by - 1,
        [functools.partial(arriving, d) for d in range(1, groups // 2 + 1)],
        outgoing, qkv, meta, out_weight, *near_blocks,
    )

    moved, got_up, got_down, got_x = lax.optimization_barrier((moved, got_up, got_down, got_x))
    last_blocks = [
        shifted(got_up[half : half + third], "head", 2),
        swapped(jnp.concatenate([got_up[third:half], got_down[: 2 * third - half]])),
        shifted(got_x[half - third : half], "head", -2),
    ]
    far_blocks = [got_up, got_down, got_x]
    att, move_prob = forward_move(meta, moved, home_att)
    far = grad_att(out_weight, far_blocks)
    part = grad_weight_part(
        meta[4:14], att, near_blocks + far_blocks, (ROWS,) * 4 + (half,) * 6
    )
    grads, send, keep = backward(
        meta, qkv, moved, att, home_prob, move_prob, near, far, out_weight, last_blocks, part
    )
    grad_weight = summed_over_groups(send, keep) * ((GROUP * groups) ** (-0.5))
    outs = apart(
        lax.all_to_all(
            grads.reshape(8, ROWS, 3 * FEAT), "head", split_axis=0, concat_axis=0, tiled=True
        )
    )
    return (*outs, grad_weight)


def solution(mesh):
    rows = P(("dp", "head"), None)
    in_specs = (rows, rows, rows, rows, P("head", None), P(), P(), P())
    out_specs = (rows, rows, rows, P("head", "dp"))
    return jax.shard_map(local, mesh=mesh, in_specs=in_specs, out_specs=out_specs, check_vma=False)
```

```python
import functools

import jax
import jax.numpy as jnp
from jax import lax
from jax.experimental import pallas as pl
from jax.experimental.pallas import tpu as pltpu
from jax.sharding import PartitionSpec as P

D = 3072
HD = 128
FEAT = 256
ROWS = 192
GROUP = 1536
HOME = 1024
MOVE = 512
HOME_MIN = 768
MOVE_MIN = 256
FAR_PIECES = (96, 128, 96, 128, 64, 64)
QB = 256
SCALE = HD ** (-0.5)
EXP2_SCALE = SCALE * 1.4426950408889634
NEG_BIG = -1e30
NN = (((1,), (0,)), ((), ()))
NT = (((1,), (1,)), ((), ()))
VMEM = pl.BlockSpec(memory_space=pltpu.VMEM)
SMEM = pl.BlockSpec(memory_space=pltpu.SMEM)
PARAMS = pltpu.CompilerParams(vmem_limit_bytes=32 * 1024 * 1024)


def dot(a, b, dims=NN):
    return lax.dot_general(a, b, dims, preferred_element_type=jnp.float32)


def flip(x):
    return x.astype(jnp.float32).T.astype(x.dtype)


def apart_kernel(packed_ref, *outs):
    for i, out in enumerate(outs):
        for j in range(4):
            out[:, j * FEAT : (j + 1) * FEAT] = packed_ref[j, :, i * FEAT : (i + 1) * FEAT]


def apart(packed):
    return pl.pallas_call(
        apart_kernel,
        grid=(2,),
        out_shape=(jax.ShapeDtypeStruct((ROWS, 8 * FEAT), jnp.bfloat16),) * 3,
        in_specs=[pl.BlockSpec((4, ROWS, 3 * FEAT), lambda i: (i, 0, 0))],
        out_specs=(pl.BlockSpec((ROWS, 4 * FEAT), lambda i: (0, i)),) * 3,
        compiler_params=PARAMS,
        name="apart",
    )(packed)


def shifted(x, axis, distance):
    n = lax.axis_size(axis)
    return lax.ppermute(x, axis, [((i - distance) % n, i) for i in range(n)])


def swapped(x):
    return lax.ppermute(x, "head", [(i, i ^ 1) for i in range(8)])


def columns(which, head):
    return pl.ds(pl.multiple_of(which * FEAT + head * HD, HD), HD)


def forward_clip(read, length, rows, sure, prob_ref, att_ref, att_first):
    def one_head(head, _):
        k = read(1, head, 0, rows)
        v_t = flip(read(2, head, 0, rows))

        def block(step, _):
            first = pl.multiple_of(step * QB, QB)
            q = read(0, head, first, QB)
            scores = dot(k, q, NT)
            key = lax.broadcasted_iota(jnp.int32, (rows - sure, QB), 0) + sure
            scores = jnp.concatenate(
                [scores[:sure], jnp.where(key < length, scores[sure:], NEG_BIG)], axis=0
            )
            peak = jnp.max(scores, axis=0, keepdims=True)
            unnorm = jnp.exp2((scores - peak) * EXP2_SCALE)
            total = jnp.sum(unnorm, axis=0, keepdims=True)
            query = lax.broadcasted_iota(jnp.int32, (1, QB), 1) + first
            prob = (unnorm * jnp.where(query < length, 1.0 / total, 0.0)).astype(jnp.bfloat16)
            prob_ref[head, :, pl.ds(first, QB)] = prob
            att = dot(v_t, prob).T.astype(jnp.bfloat16)
            there = pl.ds(pl.multiple_of(att_first + first, 128), QB)
            att_ref[there, columns(0, head)] = att
            return 0

        return lax.fori_loop(0, rows // QB, block, 0)

    lax.fori_loop(0, 2, one_head, 0)


def forward_home_kernel(meta_ref, qkv_ref, att_ref, prob_ref):
    home_first, home_len = meta_ref[0], meta_ref[1]

    def read(which, head, first, count):
        start = pl.multiple_of(home_first + first, 128)
        return qkv_ref[pl.ds(start, count), columns(which, head)]

    forward_clip(read, home_len, HOME, HOME_MIN, prob_ref, att_ref, 0)


def forward_home(meta, qkv):
    return pl.pallas_call(
        forward_home_kernel,
        out_shape=(
            jax.ShapeDtypeStruct((HOME, FEAT), jnp.bfloat16),
            jax.ShapeDtypeStruct((2, HOME, HOME), jnp.bfloat16),
        ),
        in_specs=[SMEM, VMEM],
        out_specs=(VMEM, VMEM),
        compiler_params=PARAMS,
        cost_estimate=pl.CostEstimate(
            flops=6_000_000_000, bytes_accessed=8_000_000, transcendentals=2_100_000
        ),
        name="forward_home",
    )(meta, qkv)


def forward_move_kernel(meta_ref, move_ref, home_att_ref, att_ref, prob_ref):
    home_len, arrive_len = meta_ref[1], meta_ref[2]

    def read(which, head, first, count):
        return move_ref[pl.ds(first, count), columns(which, head)]

    att_ref[:HOME, :] = home_att_ref[...]
    att_ref[HOME:, :] = jnp.zeros((GROUP - HOME, FEAT), jnp.bfloat16)
    forward_clip(read, arrive_len, MOVE, MOVE_MIN, prob_ref, att_ref, home_len)


def forward_move(meta, moved, home_att):
    return pl.pallas_call(
        forward_move_kernel,
        out_shape=(
            jax.ShapeDtypeStruct((GROUP, FEAT), jnp.bfloat16),
            jax.ShapeDtypeStruct((2, MOVE, MOVE), jnp.bfloat16),
        ),
        in_specs=[SMEM, VMEM, VMEM],
        out_specs=(VMEM, VMEM),
        compiler_params=PARAMS,
        cost_estimate=pl.CostEstimate(
            flops=150_000_000, bytes_accessed=300_000, transcendentals=50_000
        ),
        name="forward_move",
    )(meta, moved, home_att)


def grad_att_kernel(count, weight_ref, *refs):
    blocks = refs[:count]
    out_ref, acc = refs[-2:]
    step = pl.program_id(0)

    @pl.when(step == 0)
    def _():
        acc[...] = jnp.zeros_like(acc)

    dy = jnp.concatenate([block[...] for block in blocks], axis=0)
    acc[...] += dot(dy, weight_ref[...], NT)

    @pl.when(step == pl.num_programs(0) - 1)
    def _():
        out_ref[...] = acc[...].astype(jnp.bfloat16)


def grad_att(weight, blocks):
    count = len(blocks)
    total = sum(block.shape[0] for block in blocks)
    wide = D // 4
    return pl.pallas_call(
        functools.partial(grad_att_kernel, count),
        grid=(4,),
        out_shape=jax.ShapeDtypeStruct((total, FEAT), jnp.bfloat16),
        in_specs=[
            pl.BlockSpec((FEAT, wide), lambda j: (0, j)),
            *[pl.BlockSpec((block.shape[0], wide), lambda j: (0, j)) for block in blocks],
        ],
        out_specs=pl.BlockSpec((total, FEAT), lambda j: (0, 0)),
        scratch_shapes=[pltpu.VMEM((total, FEAT), jnp.float32)],
        compiler_params=PARAMS,
        cost_estimate=pl.CostEstimate(
            flops=total * 300_000, bytes_accessed=total * 650, transcendentals=0
        ),
        name="grad_att",
    )(weight, *blocks)


def place_rows(att_ref, first_ref, rows):
    picked, at = [], 0
    for count in rows:
        first = pl.multiple_of(first_ref[at], 32)
        picked.append(att_ref[pl.ds(first, count), :])
        at += 1
    return flip(jnp.concatenate(picked, axis=0))


def middle_kernel(pieces, n_far, first_ref, weight_ref, att_ref, *refs):
    blocks = refs[:-4]
    grad_att_ref, out_ref, att_t, acc = refs[-4:]
    step = pl.program_id(0)

    @pl.when(step == 0)
    def _():
        att_t[...] = place_rows(att_ref, first_ref, pieces)
        acc[...] = jnp.zeros_like(acc)

    dy = [block[...] for block in blocks]
    acc[...] += dot(jnp.concatenate(dy[-n_far:], axis=0), weight_ref[...], NT)
    out_ref[0] = dot(att_t[...], jnp.concatenate(dy, axis=0))

    @pl.when(step == pl.num_programs(0) - 1)
    def _():
        grad_att_ref[...] = acc[...].astype(jnp.bfloat16)


def middle(firsts, weight, att, near, far, pieces):
    blocks = near + far
    total = sum(pieces)
    far_rows = sum(block.shape[0] for block in far)
    wide = D // 4
    return pl.pallas_call(
        functools.partial(middle_kernel, pieces, len(far)),
        grid=(4,),
        out_shape=(
            jax.ShapeDtypeStruct((far_rows, FEAT), jnp.bfloat16),
            jax.ShapeDtypeStruct((4, FEAT, wide), jnp.float32),
        ),
        in_specs=[
            SMEM,
            pl.BlockSpec((FEAT, wide), lambda j: (0, j)),
            pl.BlockSpec((GROUP, FEAT), lambda j: (0, 0)),
            *[pl.BlockSpec((block.shape[0], wide), lambda j: (0, j)) for block in blocks],
        ],
        out_specs=(
            pl.BlockSpec((far_rows, FEAT), lambda j: (0, 0)),
            pl.BlockSpec((1, FEAT, wide), lambda j: (j, 0, 0)),
        ),
        scratch_shapes=[
            pltpu.VMEM((FEAT, total), jnp.bfloat16),
            pltpu.VMEM((far_rows, FEAT), jnp.float32),
        ],
        compiler_params=PARAMS,
        cost_estimate=pl.CostEstimate(
            flops=total * 500_000, bytes_accessed=total * 800, transcendentals=0
        ),
        name="middle",
    )(firsts, weight, att, *blocks)


def backward_clip(read, rows, prob_ref, row_first, ga_ref, att_ref, out_ref, key_acc, value_acc):
    k_t = [flip(read(1, head, 0, rows)) for head in range(2)]
    key_acc[:rows, :] = jnp.zeros((rows, FEAT), jnp.float32)
    value_acc[:rows, :] = jnp.zeros((rows, FEAT), jnp.float32)

    def block(step, _):
        first = pl.multiple_of(step * QB, QB)
        there = pl.ds(pl.multiple_of(row_first + first, 128), QB)
        for head in range(2):
            side = slice(head * HD, (head + 1) * HD)
            q = read(0, head, first, QB)
            v = read(2, head, 0, rows)
            prob = prob_ref[head, :, pl.ds(first, QB)]
            grad_att = ga_ref[there, side]
            product = grad_att.astype(jnp.float32) * att_ref[there, side].astype(jnp.float32)
            row_dot = jnp.sum(product.T, axis=0, keepdims=True)
            grad_prob = dot(v, grad_att, NT)
            grad_score = (prob.astype(jnp.float32) * (grad_prob - row_dot)).astype(jnp.bfloat16)
            value_acc[:rows, side] += dot(prob, grad_att)
            key_acc[:rows, side] += dot(grad_score, q)
            grad_query = (dot(k_t[head], grad_score) * SCALE).T.astype(jnp.bfloat16)
            out_ref[there, side] = grad_query
        return 0

    lax.fori_loop(0, rows // QB, block, 0)
    whole = pl.ds(pl.multiple_of(row_first, 128), rows)
    out_ref[whole, FEAT : 2 * FEAT] = (key_acc[:rows, :] * SCALE).astype(jnp.bfloat16)
    out_ref[whole, 2 * FEAT :] = value_acc[:rows, :].astype(jnp.bfloat16)


def backward_kernel(
    meta_ref, qkv_ref, move_ref, att_ref, home_prob_ref, move_prob_ref,
    near_ref, far_ref, weight_ref, last_a, last_b, last_c, sum_ref,
    grads_ref, send_ref, keep_ref, out_ref, ga_ref, key_acc, value_acc, done,
):
    home_first, home_len = meta_ref[0], meta_ref[1]
    half = ROWS // 2
    for i in range(4):
        first = pl.multiple_of(meta_ref[4 + i], half)
        ga_ref[pl.ds(first, ROWS), :] = near_ref[i * ROWS : (i + 1) * ROWS, :]
    at = 0
    for i, count in enumerate(FAR_PIECES):
        first = pl.multiple_of(meta_ref[8 + i], 32)
        ga_ref[pl.ds(first, count), :] = far_ref[at : at + count, :]
        at += count
    dy = jnp.concatenate([last_a[...], last_b[...], last_c[...]], axis=0)
    last = dot(dy, weight_ref[...], NT).astype(jnp.bfloat16)
    last_rows = pl.ds(pl.multiple_of(meta_ref[14], half), ROWS)
    ga_ref[last_rows, :] = last

    att_t = flip(att_ref[last_rows, :])
    wide, cut = D // 4, D // 16
    for z in range(4):
        whole = sum_ref[z] + dot(att_t, dy[:, z * wide : (z + 1) * wide])
        by_core = [
            jnp.concatenate(
                [whole[:, (2 * xh + core) * cut : (2 * xh + core + 1) * cut] for xh in range(2)],
                axis=1,
            ).astype(jnp.bfloat16)
            for core in range(2)
        ]
        first_core = meta_ref[15] == 0
        keep_ref[z] = jnp.where(first_core, by_core[0], by_core[1])
        send_ref[z] = jnp.where(first_core, by_core[1], by_core[0])

    def read_home(which, head, first, count):
        start = pl.multiple_of(home_first + first, 128)
        return qkv_ref[pl.ds(start, count), columns(which, head)]

    def read_move(which, head, first, count):
        return move_ref[pl.ds(first, count), columns(which, head)]

    out_ref[HOME:, :] = jnp.zeros((GROUP - HOME, 3 * FEAT), jnp.bfloat16)
    backward_clip(
        read_home, HOME, home_prob_ref, 0, ga_ref, att_ref, out_ref, key_acc, value_acc
    )
    start = pltpu.make_async_copy(
        out_ref.at[:HOME_MIN, :], grads_ref.at[:HOME_MIN, :], done.at[0]
    )
    start.start()
    backward_clip(
        read_move, MOVE, move_prob_ref, home_len, ga_ref, att_ref, out_ref, key_acc, value_acc
    )
    end = pltpu.make_async_copy(
        out_ref.at[HOME_MIN:, :], grads_ref.at[HOME_MIN:, :], done.at[1]
    )
    end.start()
    start.wait()
    end.wait()


def backward(meta, qkv, moved, att, home_prob, move_prob, near, far, weight, last_blocks, part):
    return pl.pallas_call(
        backward_kernel,
        out_shape=(
            pltpu.HBM((GROUP, 3 * FEAT), jnp.bfloat16),
            jax.ShapeDtypeStruct((4, FEAT, D // 8), jnp.bfloat16),
            jax.ShapeDtypeStruct((4, FEAT, D // 8), jnp.bfloat16),
        ),
        in_specs=[SMEM] + [VMEM] * 12,
        out_specs=(pl.BlockSpec(memory_space=pltpu.HBM), VMEM, VMEM),
        scratch_shapes=[
            pltpu.VMEM((GROUP, 3 * FEAT), jnp.bfloat16),
            pltpu.VMEM((GROUP, FEAT), jnp.bfloat16),
            pltpu.VMEM((HOME, FEAT), jnp.float32),
            pltpu.VMEM((HOME, FEAT), jnp.float32),
            pltpu.SemaphoreType.DMA((2,)),
        ],
        compiler_params=PARAMS,
        cost_estimate=pl.CostEstimate(
            flops=10_000_000_000, bytes_accessed=12_000_000, transcendentals=0
        ),
        name="backward",
    )(meta, qkv, moved, att, home_prob, move_prob, near, far, weight, *last_blocks, part)


def pick(x, index):
    return lax.dynamic_index_in_dim(x, index, 0, keepdims=False)


def summed_over_groups(send, keep):
    group_id = lax.axis_index("dp")
    z, xh = group_id // 4, group_id // 2 % 2
    got = lax.ppermute(send, "dp", [(i, i ^ 1) for i in range(16)])
    both = (keep.astype(jnp.float32) + got.astype(jnp.float32)).astype(jnp.bfloat16)
    total = pick(both, z).astype(jnp.float32)
    for distance in (1, 2, 3):
        sent = pick(both, (z + distance) % 4)
        total = total + shifted(sent, "dp", 4 * distance).astype(jnp.float32)
    low, high = total[:, : D // 16], total[:, D // 16 :]
    sent = jnp.where(xh == 0, high, low).astype(jnp.bfloat16)
    got = lax.ppermute(sent, "dp", [(i, i ^ 2) for i in range(16)])
    return jnp.where(xh == 0, low, high) + got.astype(jnp.float32)


def arriving(distance, outgoing, qkv, meta, weight, *blocks):
    moved = shifted(outgoing, "dp", distance)
    home_att, home_prob = forward_home(meta, qkv)
    near = grad_att(weight, blocks)
    return moved, home_att, home_prob, near


def local(query_rows, key_rows, value_rows, out_grad, out_weight, clip_len, clip_group, clip_start):
    groups = lax.axis_size("dp")
    group_id = lax.axis_index("dp")
    me = lax.axis_index("head")
    rotate_by = jnp.mod(clip_group[1] - clip_group[0], groups)
    source_group = jnp.mod(group_id - rotate_by, groups)
    half, third = ROWS // 2, ROWS // 3

    up, down = ((me + 6) % 8) * ROWS, ((me + 2) % 8) * ROWS
    far_a = ((me + 4) % 8) * ROWS
    far_b, far_c = (((me + 2) % 8) ^ 1) * ROWS, (((me + 6) % 8) ^ 1) * ROWS
    far_d = (((me + 4) % 8) ^ 1) * ROWS
    meta = jnp.stack(
        [
            clip_start[2 * group_id],
            clip_len[2 * group_id],
            clip_len[2 * source_group + 1],
            jnp.int32(0),
            me * ROWS,
            (me ^ 1) * ROWS,
            up,
            down,
            far_a,
            far_c,
            far_a + half,
            far_b + third,
            far_b,
            far_c + 2 * third,
            far_d,
            group_id % 2,
        ]
    ).astype(jnp.int32)

    dy_x = swapped(out_grad)
    dy_up = shifted(out_grad, "head", 2)
    dy_down = shifted(out_grad, "head", -2)

    packed = jnp.concatenate(
        [x.reshape(ROWS, 8, FEAT) for x in (query_rows, key_rows, value_rows)], axis=2
    )
    qkv = lax.all_to_all(packed, "head", split_axis=1, concat_axis=0, tiled=False)
    qkv = qkv.reshape(GROUP, 3 * FEAT)
    padded = jnp.concatenate([qkv, jnp.zeros((MOVE // 2, 3 * FEAT), jnp.bfloat16)], axis=0)
    outgoing = lax.dynamic_slice_in_dim(padded, clip_start[2 * group_id + 1], MOVE, 0)

    got_up = shifted(jnp.concatenate([dy_up[:half], dy_x[: 2 * third]]), "head", 2)
    got_down = shifted(jnp.concatenate([dy_down[half:], dy_x[third:]]), "head", -2)
    got_x = swapped(jnp.concatenate([dy_down[:third], dy_up[2 * third :]]))

    near_blocks = [out_grad, dy_x, dy_up, dy_down]
    moved, home_att, home_prob, near = lax.switch(
        rotate_by - 1,
        [functools.partial(arriving, d) for d in range(1, groups // 2 + 1)],
        outgoing, qkv, meta, out_weight, *near_blocks,
    )

    moved, got_up, got_down, got_x = lax.optimization_barrier((moved, got_up, got_down, got_x))
    last_blocks = [
        shifted(got_up[half : half + third], "head", 2),
        swapped(jnp.concatenate([got_up[third:half], got_down[: 2 * third - half]])),
        shifted(got_down[-third:], "head", -2),
    ]
    far_blocks = [got_up, got_down, got_x]
    att, move_prob = forward_move(meta, moved, home_att)
    far, part = middle(
        meta[4:14], out_weight, att, near_blocks, far_blocks, (ROWS,) * 4 + FAR_PIECES
    )
    grads, send, keep = backward(
        meta, qkv, moved, att, home_prob, move_prob, near, far, out_weight, last_blocks, part
    )
    grad_weight = summed_over_groups(send, keep) * ((GROUP * groups) ** (-0.5))
    outs = apart(
        lax.all_to_all(
            grads.reshape(8, ROWS, 3 * FEAT), "head", split_axis=0, concat_axis=0, tiled=True
        )
    )
    return (*outs, grad_weight)


def solution(mesh):
    rows = P(("dp", "head"), None)
    in_specs = (rows, rows, rows, rows, P("head", None), P(), P(), P())
    out_specs = (rows, rows, rows, P("head", "dp"))
    return jax.shard_map(local, mesh=mesh, in_specs=in_specs, out_specs=out_specs, check_vma=False)
```

```python
import functools

import jax
import jax.numpy as jnp
from jax import lax
from jax.experimental import pallas as pl
from jax.experimental.pallas import tpu as pltpu
from jax.sharding import PartitionSpec as P

D = 3072
HD = 128
FEAT = 256
ROWS = 192
GROUP = 1536
HOME = 1024
MOVE = 512
HOME_MIN = 768
MOVE_MIN = 256
FAR_PIECES = (96, 128, 96, 128, 64, 64)
QB = 256
SCALE = HD ** (-0.5)
EXP2_SCALE = SCALE * 1.4426950408889634
NEG_BIG = -1e30
NN = (((1,), (0,)), ((), ()))
NT = (((1,), (1,)), ((), ()))
VMEM = pl.BlockSpec(memory_space=pltpu.VMEM)
SMEM = pl.BlockSpec(memory_space=pltpu.SMEM)
PARAMS = pltpu.CompilerParams(vmem_limit_bytes=32 * 1024 * 1024)


def dot(a, b, dims=NN):
    return lax.dot_general(a, b, dims, preferred_element_type=jnp.float32)


def flip(x):
    return x.astype(jnp.float32).T.astype(x.dtype)


def apart_kernel(packed_ref, *outs):
    for i, out in enumerate(outs):
        for j in range(4):
            out[:, j * FEAT : (j + 1) * FEAT] = packed_ref[j, :, i * FEAT : (i + 1) * FEAT]


def apart(packed):
    return pl.pallas_call(
        apart_kernel,
        grid=(2,),
        out_shape=(jax.ShapeDtypeStruct((ROWS, 8 * FEAT), jnp.bfloat16),) * 3,
        in_specs=[pl.BlockSpec((4, ROWS, 3 * FEAT), lambda i: (i, 0, 0))],
        out_specs=(pl.BlockSpec((ROWS, 4 * FEAT), lambda i: (0, i)),) * 3,
        compiler_params=PARAMS,
        name="apart",
    )(packed)


def shifted(x, axis, distance):
    n = lax.axis_size(axis)
    return lax.ppermute(x, axis, [((i - distance) % n, i) for i in range(n)])


def swapped(x):
    return lax.ppermute(x, "head", [(i, i ^ 1) for i in range(8)])


def columns(which, head):
    return pl.ds(pl.multiple_of(which * FEAT + head * HD, HD), HD)


def forward_clip(read, length, rows, sure, prob_ref, att_ref, att_first):
    def one_head(head, _):
        k = read(1, head, 0, rows)
        v_t = flip(read(2, head, 0, rows))

        def block(step, _):
            first = pl.multiple_of(step * QB, QB)
            q = read(0, head, first, QB)
            scores = dot(k, q, NT)
            key = lax.broadcasted_iota(jnp.int32, (rows - sure, QB), 0) + sure
            scores = jnp.concatenate(
                [scores[:sure], jnp.where(key < length, scores[sure:], NEG_BIG)], axis=0
            )
            peak = jnp.max(scores, axis=0, keepdims=True)
            unnorm = jnp.exp2((scores - peak) * EXP2_SCALE)
            total = jnp.sum(unnorm, axis=0, keepdims=True)
            query = lax.broadcasted_iota(jnp.int32, (1, QB), 1) + first
            prob = (unnorm * jnp.where(query < length, 1.0 / total, 0.0)).astype(jnp.bfloat16)
            prob_ref[head, :, pl.ds(first, QB)] = prob
            att = dot(v_t, prob).T.astype(jnp.bfloat16)
            there = pl.ds(pl.multiple_of(att_first + first, 128), QB)
            att_ref[there, columns(0, head)] = att
            return 0

        return lax.fori_loop(0, rows // QB, block, 0)

    lax.fori_loop(0, 2, one_head, 0)


def forward_home_kernel(meta_ref, qkv_ref, att_ref, prob_ref):
    home_first, home_len = meta_ref[0], meta_ref[1]

    def read(which, head, first, count):
        start = pl.multiple_of(home_first + first, 128)
        return qkv_ref[pl.ds(start, count), columns(which, head)]

    forward_clip(read, home_len, HOME, HOME_MIN, prob_ref, att_ref, 0)


def forward_home(meta, qkv):
    return pl.pallas_call(
        forward_home_kernel,
        out_shape=(
            jax.ShapeDtypeStruct((HOME, FEAT), jnp.bfloat16),
            jax.ShapeDtypeStruct((2, HOME, HOME), jnp.bfloat16),
        ),
        in_specs=[SMEM, VMEM],
        out_specs=(VMEM, VMEM),
        compiler_params=PARAMS,
        cost_estimate=pl.CostEstimate(
            flops=6_000_000_000, bytes_accessed=8_000_000, transcendentals=2_100_000
        ),
        name="forward_home",
    )(meta, qkv)


def grad_att_kernel(count, weight_ref, *refs):
    blocks = refs[:count]
    out_ref, acc = refs[-2:]
    step = pl.program_id(0)

    @pl.when(step == 0)
    def _():
        acc[...] = jnp.zeros_like(acc)

    dy = jnp.concatenate([block[...] for block in blocks], axis=0)
    acc[...] += dot(dy, weight_ref[...], NT)

    @pl.when(step == pl.num_programs(0) - 1)
    def _():
        out_ref[...] = acc[...].astype(jnp.bfloat16)


def grad_att(weight, blocks):
    count = len(blocks)
    total = sum(block.shape[0] for block in blocks)
    wide = D // 4
    return pl.pallas_call(
        functools.partial(grad_att_kernel, count),
        grid=(4,),
        out_shape=jax.ShapeDtypeStruct((total, FEAT), jnp.bfloat16),
        in_specs=[
            pl.BlockSpec((FEAT, wide), lambda j: (0, j)),
            *[pl.BlockSpec((block.shape[0], wide), lambda j: (0, j)) for block in blocks],
        ],
        out_specs=pl.BlockSpec((total, FEAT), lambda j: (0, 0)),
        scratch_shapes=[pltpu.VMEM((total, FEAT), jnp.float32)],
        compiler_params=PARAMS,
        cost_estimate=pl.CostEstimate(
            flops=total * 300_000, bytes_accessed=total * 650, transcendentals=0
        ),
        name="grad_att",
    )(weight, *blocks)


def middle_kernel(pieces, n_far, meta_ref, move_ref, home_att_ref, weight_ref, *refs):
    blocks = refs[:-6]
    att_ref, prob_ref, grad_att_ref, out_ref, att_t, acc = refs[-6:]
    step = pl.program_id(0)

    def read(which, head, first, count):
        return move_ref[pl.ds(first, count), columns(which, head)]

    @pl.when(step == 0)
    def _():
        att_ref[:HOME, :] = home_att_ref[...]
        att_ref[HOME:, :] = jnp.zeros((GROUP - HOME, FEAT), jnp.bfloat16)
        forward_clip(read, meta_ref[2], MOVE, MOVE_MIN, prob_ref, att_ref, meta_ref[1])
        picked = [
            att_ref[pl.ds(pl.multiple_of(meta_ref[4 + i], 32), count), :]
            for i, count in enumerate(pieces)
        ]
        att_t[...] = flip(jnp.concatenate(picked, axis=0))
        acc[...] = jnp.zeros_like(acc)

    dy = [block[...] for block in blocks]
    acc[...] += dot(jnp.concatenate(dy[-n_far:], axis=0), weight_ref[...], NT)
    out_ref[0] = dot(att_t[...], jnp.concatenate(dy, axis=0))

    @pl.when(step == pl.num_programs(0) - 1)
    def _():
        grad_att_ref[...] = acc[...].astype(jnp.bfloat16)


def middle(meta, moved, home_att, weight, near, far, pieces):
    blocks = near + far
    total = sum(pieces)
    far_rows = sum(block.shape[0] for block in far)
    wide = D // 4
    return pl.pallas_call(
        functools.partial(middle_kernel, pieces, len(far)),
        grid=(4,),
        out_shape=(
            jax.ShapeDtypeStruct((GROUP, FEAT), jnp.bfloat16),
            jax.ShapeDtypeStruct((2, MOVE, MOVE), jnp.bfloat16),
            jax.ShapeDtypeStruct((far_rows, FEAT), jnp.bfloat16),
            jax.ShapeDtypeStruct((4, FEAT, wide), jnp.float32),
        ),
        in_specs=[
            SMEM,
            VMEM,
            VMEM,
            pl.BlockSpec((FEAT, wide), lambda j: (0, j)),
            *[pl.BlockSpec((block.shape[0], wide), lambda j: (0, j)) for block in blocks],
        ],
        out_specs=(
            VMEM,
            VMEM,
            pl.BlockSpec((far_rows, FEAT), lambda j: (0, 0)),
            pl.BlockSpec((1, FEAT, wide), lambda j: (j, 0, 0)),
        ),
        scratch_shapes=[
            pltpu.VMEM((FEAT, total), jnp.bfloat16),
            pltpu.VMEM((far_rows, FEAT), jnp.float32),
        ],
        compiler_params=PARAMS,
        cost_estimate=pl.CostEstimate(
            flops=total * 600_000, bytes_accessed=total * 1_000, transcendentals=0
        ),
        name="middle",
    )(meta, moved, home_att, weight, *blocks)


def backward_clip(read, rows, prob_ref, row_first, ga_ref, att_ref, out_ref, key_acc, value_acc):
    k_t = [flip(read(1, head, 0, rows)) for head in range(2)]
    key_acc[:rows, :] = jnp.zeros((rows, FEAT), jnp.float32)
    value_acc[:rows, :] = jnp.zeros((rows, FEAT), jnp.float32)

    def block(step, _):
        first = pl.multiple_of(step * QB, QB)
        there = pl.ds(pl.multiple_of(row_first + first, 128), QB)
        for head in range(2):
            side = slice(head * HD, (head + 1) * HD)
            q = read(0, head, first, QB)
            v = read(2, head, 0, rows)
            prob = prob_ref[head, :, pl.ds(first, QB)]
            grad_att = ga_ref[there, side]
            product = grad_att.astype(jnp.float32) * att_ref[there, side].astype(jnp.float32)
            row_dot = jnp.sum(product.T, axis=0, keepdims=True)
            grad_prob = dot(v, grad_att, NT)
            grad_score = (prob.astype(jnp.float32) * (grad_prob - row_dot)).astype(jnp.bfloat16)
            value_acc[:rows, side] += dot(prob, grad_att)
            key_acc[:rows, side] += dot(grad_score, q)
            grad_query = (dot(k_t[head], grad_score) * SCALE).T.astype(jnp.bfloat16)
            out_ref[there, side] = grad_query
        return 0

    lax.fori_loop(0, rows // QB, block, 0)
    whole = pl.ds(pl.multiple_of(row_first, 128), rows)
    out_ref[whole, FEAT : 2 * FEAT] = (key_acc[:rows, :] * SCALE).astype(jnp.bfloat16)
    out_ref[whole, 2 * FEAT :] = value_acc[:rows, :].astype(jnp.bfloat16)


def backward_kernel(
    meta_ref, qkv_ref, move_ref, att_ref, home_prob_ref, move_prob_ref,
    near_ref, far_ref, weight_ref, last_a, last_b, last_c, sum_ref,
    grads_ref, send_ref, keep_ref, out_ref, ga_ref, key_acc, value_acc, done,
):
    home_first, home_len = meta_ref[0], meta_ref[1]
    half = ROWS // 2
    for i in range(4):
        first = pl.multiple_of(meta_ref[4 + i], half)
        ga_ref[pl.ds(first, ROWS), :] = near_ref[i * ROWS : (i + 1) * ROWS, :]
    at = 0
    for i, count in enumerate(FAR_PIECES):
        first = pl.multiple_of(meta_ref[8 + i], 32)
        ga_ref[pl.ds(first, count), :] = far_ref[at : at + count, :]
        at += count
    dy = jnp.concatenate([last_a[...], last_b[...], last_c[...]], axis=0)
    last = dot(dy, weight_ref[...], NT).astype(jnp.bfloat16)
    last_rows = pl.ds(pl.multiple_of(meta_ref[14], half), ROWS)
    ga_ref[last_rows, :] = last

    att_t = flip(att_ref[last_rows, :])
    wide, cut = D // 4, D // 16
    for z in range(4):
        whole = sum_ref[z] + dot(att_t, dy[:, z * wide : (z + 1) * wide])
        by_core = [
            jnp.concatenate(
                [whole[:, (2 * xh + core) * cut : (2 * xh + core + 1) * cut] for xh in range(2)],
                axis=1,
            ).astype(jnp.bfloat16)
            for core in range(2)
        ]
        first_core = meta_ref[15] == 0
        keep_ref[z] = jnp.where(first_core, by_core[0], by_core[1])
        send_ref[z] = jnp.where(first_core, by_core[1], by_core[0])

    def read_home(which, head, first, count):
        start = pl.multiple_of(home_first + first, 128)
        return qkv_ref[pl.ds(start, count), columns(which, head)]

    def read_move(which, head, first, count):
        return move_ref[pl.ds(first, count), columns(which, head)]

    out_ref[HOME:, :] = jnp.zeros((GROUP - HOME, 3 * FEAT), jnp.bfloat16)
    backward_clip(
        read_home, HOME, home_prob_ref, 0, ga_ref, att_ref, out_ref, key_acc, value_acc
    )
    start = pltpu.make_async_copy(
        out_ref.at[:HOME_MIN, :], grads_ref.at[:HOME_MIN, :], done.at[0]
    )
    start.start()
    backward_clip(
        read_move, MOVE, move_prob_ref, home_len, ga_ref, att_ref, out_ref, key_acc, value_acc
    )
    end = pltpu.make_async_copy(
        out_ref.at[HOME_MIN:, :], grads_ref.at[HOME_MIN:, :], done.at[1]
    )
    end.start()
    start.wait()
    end.wait()


def backward(meta, qkv, moved, att, home_prob, move_prob, near, far, weight, last_blocks, part):
    return pl.pallas_call(
        backward_kernel,
        out_shape=(
            pltpu.HBM((GROUP, 3 * FEAT), jnp.bfloat16),
            jax.ShapeDtypeStruct((4, FEAT, D // 8), jnp.bfloat16),
            jax.ShapeDtypeStruct((4, FEAT, D // 8), jnp.bfloat16),
        ),
        in_specs=[SMEM] + [VMEM] * 12,
        out_specs=(pl.BlockSpec(memory_space=pltpu.HBM), VMEM, VMEM),
        scratch_shapes=[
            pltpu.VMEM((GROUP, 3 * FEAT), jnp.bfloat16),
            pltpu.VMEM((GROUP, FEAT), jnp.bfloat16),
            pltpu.VMEM((HOME, FEAT), jnp.float32),
            pltpu.VMEM((HOME, FEAT), jnp.float32),
            pltpu.SemaphoreType.DMA((2,)),
        ],
        compiler_params=PARAMS,
        cost_estimate=pl.CostEstimate(
            flops=10_000_000_000, bytes_accessed=12_000_000, transcendentals=0
        ),
        name="backward",
    )(meta, qkv, moved, att, home_prob, move_prob, near, far, weight, *last_blocks, part)


def pick(x, index):
    return lax.dynamic_index_in_dim(x, index, 0, keepdims=False)


def summed_over_groups(send, keep):
    group_id = lax.axis_index("dp")
    z, xh = group_id // 4, group_id // 2 % 2
    got = lax.ppermute(send, "dp", [(i, i ^ 1) for i in range(16)])
    both = (keep.astype(jnp.float32) + got.astype(jnp.float32)).astype(jnp.bfloat16)
    total = pick(both, z).astype(jnp.float32)
    for distance in (1, 2, 3):
        sent = pick(both, (z + distance) % 4)
        total = total + shifted(sent, "dp", 4 * distance).astype(jnp.float32)
    low, high = total[:, : D // 16], total[:, D // 16 :]
    sent = jnp.where(xh == 0, high, low).astype(jnp.bfloat16)
    got = lax.ppermute(sent, "dp", [(i, i ^ 2) for i in range(16)])
    return jnp.where(xh == 0, low, high) + got.astype(jnp.float32)


def arriving(distance, outgoing, qkv, meta, weight, *blocks):
    moved = shifted(outgoing, "dp", distance)
    home_att, home_prob = forward_home(meta, qkv)
    near = grad_att(weight, blocks)
    return moved, home_att, home_prob, near


def local(query_rows, key_rows, value_rows, out_grad, out_weight, clip_len, clip_group, clip_start):
    groups = lax.axis_size("dp")
    group_id = lax.axis_index("dp")
    me = lax.axis_index("head")
    rotate_by = jnp.mod(clip_group[1] - clip_group[0], groups)
    source_group = jnp.mod(group_id - rotate_by, groups)
    half, third = ROWS // 2, ROWS // 3

    up, down = ((me + 6) % 8) * ROWS, ((me + 2) % 8) * ROWS
    far_a = ((me + 4) % 8) * ROWS
    far_b, far_c = (((me + 2) % 8) ^ 1) * ROWS, (((me + 6) % 8) ^ 1) * ROWS
    far_d = (((me + 4) % 8) ^ 1) * ROWS
    meta = jnp.stack(
        [
            clip_start[2 * group_id],
            clip_len[2 * group_id],
            clip_len[2 * source_group + 1],
            jnp.int32(0),
            me * ROWS,
            (me ^ 1) * ROWS,
            up,
            down,
            far_a,
            far_c,
            far_a + half,
            far_b + third,
            far_b,
            far_c + 2 * third,
            far_d,
            group_id % 2,
        ]
    ).astype(jnp.int32)

    dy_x = swapped(out_grad)
    dy_up = shifted(out_grad, "head", 2)
    dy_down = shifted(out_grad, "head", -2)

    packed = jnp.concatenate(
        [x.reshape(ROWS, 8, FEAT) for x in (query_rows, key_rows, value_rows)], axis=2
    )
    qkv = lax.all_to_all(packed, "head", split_axis=1, concat_axis=0, tiled=False)
    qkv = qkv.reshape(GROUP, 3 * FEAT)
    padded = jnp.concatenate([qkv, jnp.zeros((MOVE // 2, 3 * FEAT), jnp.bfloat16)], axis=0)
    outgoing = lax.dynamic_slice_in_dim(padded, clip_start[2 * group_id + 1], MOVE, 0)

    got_up = shifted(jnp.concatenate([dy_up[:half], dy_x[: 2 * third]]), "head", 2)
    got_down = shifted(jnp.concatenate([dy_down[half:], dy_x[third:]]), "head", -2)
    got_x = swapped(jnp.concatenate([dy_down[:third], dy_up[2 * third :]]))

    near_blocks = [out_grad, dy_x, dy_up, dy_down]
    moved, home_att, home_prob, near = lax.switch(
        rotate_by - 1,
        [functools.partial(arriving, d) for d in range(1, groups // 2 + 1)],
        outgoing, qkv, meta, out_weight, *near_blocks,
    )

    moved, got_up, got_down, got_x = lax.optimization_barrier((moved, got_up, got_down, got_x))
    last_blocks = [
        shifted(got_up[half : half + third], "head", 2),
        swapped(jnp.concatenate([got_up[third:half], got_down[: 2 * third - half]])),
        shifted(got_down[-third:], "head", -2),
    ]
    far_blocks = [got_up, got_down, got_x]
    att, move_prob, far, part = middle(
        meta, moved, home_att, out_weight, near_blocks, far_blocks, (ROWS,) * 4 + FAR_PIECES
    )
    grads, send, keep = backward(
        meta, qkv, moved, att, home_prob, move_prob, near, far, out_weight, last_blocks, part
    )
    grad_weight = summed_over_groups(send, keep) * ((GROUP * groups) ** (-0.5))
    outs = apart(
        lax.all_to_all(
            grads.reshape(8, ROWS, 3 * FEAT), "head", split_axis=0, concat_axis=0, tiled=True
        )
    )
    return (*outs, grad_weight)


def solution(mesh):
    rows = P(("dp", "head"), None)
    in_specs = (rows, rows, rows, rows, P("head", None), P(), P(), P())
    out_specs = (rows, rows, rows, P("head", "dp"))
    return jax.shard_map(local, mesh=mesh, in_specs=in_specs, out_specs=out_specs, check_vma=False)
```

```python
import functools

import jax
import jax.numpy as jnp
from jax import lax
from jax.experimental import pallas as pl
from jax.experimental.pallas import tpu as pltpu
from jax.sharding import PartitionSpec as P

D = 3072
HD = 128
FEAT = 256
ROWS = 192
GROUP = 1536
HOME = 1024
MOVE = 512
HOME_MIN = 768
MOVE_MIN = 256
FAR_PIECES = (96, 128, 96, 128, 64, 64)
QB = 256
BQ = 512
SCALE = HD ** (-0.5)
EXP2_SCALE = SCALE * 1.4426950408889634
NEG_BIG = -1e30
NN = (((1,), (0,)), ((), ()))
NT = (((1,), (1,)), ((), ()))
VMEM = pl.BlockSpec(memory_space=pltpu.VMEM)
SMEM = pl.BlockSpec(memory_space=pltpu.SMEM)
HBM = pl.BlockSpec(memory_space=pltpu.HBM)
PARAMS = pltpu.CompilerParams(vmem_limit_bytes=32 * 1024 * 1024)


def dot(a, b, dims=NN):
    return lax.dot_general(a, b, dims, preferred_element_type=jnp.float32)


def flip(x):
    return x.astype(jnp.float32).T.astype(x.dtype)


def apart_kernel(packed_ref, *outs):
    for i, out in enumerate(outs):
        for j in range(4):
            out[:, j * FEAT : (j + 1) * FEAT] = packed_ref[j, :, i * FEAT : (i + 1) * FEAT]


def apart(packed):
    return pl.pallas_call(
        apart_kernel,
        grid=(2,),
        out_shape=(jax.ShapeDtypeStruct((ROWS, 8 * FEAT), jnp.bfloat16),) * 3,
        in_specs=[pl.BlockSpec((4, ROWS, 3 * FEAT), lambda i: (i, 0, 0))],
        out_specs=(pl.BlockSpec((ROWS, 4 * FEAT), lambda i: (0, i)),) * 3,
        compiler_params=PARAMS,
        name="apart",
    )(packed)


def shifted(x, axis, distance):
    n = lax.axis_size(axis)
    return lax.ppermute(x, axis, [((i - distance) % n, i) for i in range(n)])


def swapped(x):
    return lax.ppermute(x, "head", [(i, i ^ 1) for i in range(8)])


def columns(which, head):
    return pl.ds(pl.multiple_of(which * FEAT + head * HD, HD), HD)


def forward_clip(read, length, rows, sure, prob_ref, att_ref, att_first):
    def one_head(head, _):
        k = read(1, head, 0, rows)
        v_t = flip(read(2, head, 0, rows))

        def block(step, _):
            first = pl.multiple_of(step * QB, QB)
            q = read(0, head, first, QB)
            scores = dot(k, q, NT)
            key = lax.broadcasted_iota(jnp.int32, (rows - sure, QB), 0) + sure
            scores = jnp.concatenate(
                [scores[:sure], jnp.where(key < length, scores[sure:], NEG_BIG)], axis=0
            )
            peak = jnp.max(scores, axis=0, keepdims=True)
            unnorm = jnp.exp2((scores - peak) * EXP2_SCALE)
            total = jnp.sum(unnorm, axis=0, keepdims=True)
            query = lax.broadcasted_iota(jnp.int32, (1, QB), 1) + first
            prob = (unnorm * jnp.where(query < length, 1.0 / total, 0.0)).astype(jnp.bfloat16)
            prob_ref[head, :, pl.ds(first, QB)] = prob
            att = dot(v_t, prob).T.astype(jnp.bfloat16)
            there = pl.ds(pl.multiple_of(att_first + first, 128), QB)
            att_ref[there, columns(0, head)] = att
            return 0

        return lax.fori_loop(0, rows // QB, block, 0)

    lax.fori_loop(0, 2, one_head, 0)


def forward_home_kernel(meta_ref, qkv_ref, att_ref, prob_ref):
    home_first, home_len = meta_ref[0], meta_ref[1]

    def read(which, head, first, count):
        start = pl.multiple_of(home_first + first, 128)
        return qkv_ref[pl.ds(start, count), columns(which, head)]

    forward_clip(read, home_len, HOME, HOME_MIN, prob_ref, att_ref, 0)


def forward_home(meta, qkv):
    return pl.pallas_call(
        forward_home_kernel,
        out_shape=(
            jax.ShapeDtypeStruct((HOME, FEAT), jnp.bfloat16),
            jax.ShapeDtypeStruct((2, HOME, HOME), jnp.bfloat16),
        ),
        in_specs=[SMEM, VMEM],
        out_specs=(VMEM, VMEM),
        compiler_params=PARAMS,
        cost_estimate=pl.CostEstimate(
            flops=6_000_000_000, bytes_accessed=8_000_000, transcendentals=2_100_000
        ),
        name="forward_home",
    )(meta, qkv)


def grad_att_kernel(count, weight_ref, *refs):
    blocks = refs[:count]
    out_ref, acc = refs[-2:]
    step = pl.program_id(0)

    @pl.when(step == 0)
    def _():
        acc[...] = jnp.zeros_like(acc)

    dy = jnp.concatenate([block[...] for block in blocks], axis=0)
    acc[...] += dot(dy, weight_ref[...], NT)

    @pl.when(step == pl.num_programs(0) - 1)
    def _():
        out_ref[...] = acc[...].astype(jnp.bfloat16)


def grad_att(weight, blocks):
    count = len(blocks)
    total = sum(block.shape[0] for block in blocks)
    wide = D // 4
    return pl.pallas_call(
        functools.partial(grad_att_kernel, count),
        grid=(4,),
        out_shape=jax.ShapeDtypeStruct((total, FEAT), jnp.bfloat16),
        in_specs=[
            pl.BlockSpec((FEAT, wide), lambda j: (0, j)),
            *[pl.BlockSpec((block.shape[0], wide), lambda j: (0, j)) for block in blocks],
        ],
        out_specs=pl.BlockSpec((total, FEAT), lambda j: (0, 0)),
        scratch_shapes=[pltpu.VMEM((total, FEAT), jnp.float32)],
        compiler_params=PARAMS,
        cost_estimate=pl.CostEstimate(
            flops=total * 300_000, bytes_accessed=total * 650, transcendentals=0
        ),
        name="grad_att",
    )(weight, *blocks)


def middle_kernel(pieces, n_far, meta_ref, move_ref, home_att_ref, weight_ref, *refs):
    blocks = refs[:-6]
    att_ref, prob_ref, grad_att_ref, out_ref, att_t, acc = refs[-6:]
    step = pl.program_id(0)

    def read(which, head, first, count):
        return move_ref[pl.ds(first, count), columns(which, head)]

    @pl.when(step == 0)
    def _():
        att_ref[:HOME, :] = home_att_ref[...]
        att_ref[HOME:, :] = jnp.zeros((GROUP - HOME, FEAT), jnp.bfloat16)
        forward_clip(read, meta_ref[2], MOVE, MOVE_MIN, prob_ref, att_ref, meta_ref[1])
        picked = [
            att_ref[pl.ds(pl.multiple_of(meta_ref[4 + i], 32), count), :]
            for i, count in enumerate(pieces)
        ]
        att_t[...] = flip(jnp.concatenate(picked, axis=0))
        acc[...] = jnp.zeros_like(acc)

    dy = [block[...] for block in blocks]
    acc[...] += dot(jnp.concatenate(dy[-n_far:], axis=0), weight_ref[...], NT)
    out_ref[0] = dot(att_t[...], jnp.concatenate(dy, axis=0))

    @pl.when(step == pl.num_programs(0) - 1)
    def _():
        grad_att_ref[...] = acc[...].astype(jnp.bfloat16)


def middle(meta, moved, home_att, weight, near, far, pieces):
    blocks = near + far
    total = sum(pieces)
    far_rows = sum(block.shape[0] for block in far)
    wide = D // 4
    return pl.pallas_call(
        functools.partial(middle_kernel, pieces, len(far)),
        grid=(4,),
        out_shape=(
            jax.ShapeDtypeStruct((GROUP, FEAT), jnp.bfloat16),
            jax.ShapeDtypeStruct((2, MOVE, MOVE), jnp.bfloat16),
            jax.ShapeDtypeStruct((far_rows, FEAT), jnp.bfloat16),
            jax.ShapeDtypeStruct((4, FEAT, wide), jnp.float32),
        ),
        in_specs=[
            SMEM,
            VMEM,
            VMEM,
            pl.BlockSpec((FEAT, wide), lambda j: (0, j)),
            *[pl.BlockSpec((block.shape[0], wide), lambda j: (0, j)) for block in blocks],
        ],
        out_specs=(
            VMEM,
            VMEM,
            pl.BlockSpec((far_rows, FEAT), lambda j: (0, 0)),
            pl.BlockSpec((1, FEAT, wide), lambda j: (j, 0, 0)),
        ),
        scratch_shapes=[
            pltpu.VMEM((FEAT, total), jnp.bfloat16),
            pltpu.VMEM((far_rows, FEAT), jnp.float32),
        ],
        compiler_params=PARAMS,
        cost_estimate=pl.CostEstimate(
            flops=total * 600_000, bytes_accessed=total * 1_000, transcendentals=0
        ),
        name="middle",
    )(meta, moved, home_att, weight, *blocks)


def backward_clip(read, rows, prob_ref, row_first, ga_ref, att_ref, out_ref, key_acc, value_acc):
    k_t = [flip(read(1, head, 0, rows)) for head in range(2)]
    key_acc[:rows, :] = jnp.zeros((rows, FEAT), jnp.float32)
    value_acc[:rows, :] = jnp.zeros((rows, FEAT), jnp.float32)

    def block(step, _):
        first = pl.multiple_of(step * BQ, BQ)
        there = pl.ds(pl.multiple_of(row_first + first, 128), BQ)
        for head in range(2):
            side = slice(head * HD, (head + 1) * HD)
            q = read(0, head, first, BQ)
            v = read(2, head, 0, rows)
            prob = prob_ref[head, :, pl.ds(first, BQ)]
            grad_att = ga_ref[there, side]
            product = grad_att.astype(jnp.float32) * att_ref[there, side].astype(jnp.float32)
            row_dot = jnp.sum(product.T, axis=0, keepdims=True)
            grad_prob = dot(v, grad_att, NT)
            grad_score = (prob.astype(jnp.float32) * (grad_prob - row_dot)).astype(jnp.bfloat16)
            value_acc[:rows, side] += dot(prob, grad_att)
            key_acc[:rows, side] += dot(grad_score, q)
            grad_query = (dot(k_t[head], grad_score) * SCALE).T.astype(jnp.bfloat16)
            out_ref[there, side] = grad_query
        return 0

    lax.fori_loop(0, rows // BQ, block, 0)
    whole = pl.ds(pl.multiple_of(row_first, 128), rows)
    out_ref[whole, FEAT : 2 * FEAT] = (key_acc[:rows, :] * SCALE).astype(jnp.bfloat16)
    out_ref[whole, 2 * FEAT :] = value_acc[:rows, :].astype(jnp.bfloat16)


def backward_kernel(
    meta_ref, qkv_ref, move_ref, att_ref, home_prob_ref, move_prob_ref,
    near_ref, far_ref, weight_ref, last_a, last_b, last_c, sum_ref,
    grads_ref, send_ref, keep_ref, out_ref, ga_ref, key_acc, value_acc, sent_ref, done,
):
    home_first, home_len = meta_ref[0], meta_ref[1]
    half = ROWS // 2
    for i in range(4):
        first = pl.multiple_of(meta_ref[4 + i], half)
        ga_ref[pl.ds(first, ROWS), :] = near_ref[i * ROWS : (i + 1) * ROWS, :]
    at = 0
    for i, count in enumerate(FAR_PIECES):
        first = pl.multiple_of(meta_ref[8 + i], 32)
        ga_ref[pl.ds(first, count), :] = far_ref[at : at + count, :]
        at += count
    dy = jnp.concatenate([last_a[...], last_b[...], last_c[...]], axis=0)
    last = dot(dy, weight_ref[...], NT).astype(jnp.bfloat16)
    last_rows = pl.ds(pl.multiple_of(meta_ref[14], half), ROWS)
    ga_ref[last_rows, :] = last

    att_t = flip(att_ref[last_rows, :])
    wide, cut = D // 4, D // 16
    for z in range(4):
        whole = sum_ref[z] + dot(att_t, dy[:, z * wide : (z + 1) * wide])
        by_core = [
            jnp.concatenate(
                [whole[:, (2 * xh + core) * cut : (2 * xh + core + 1) * cut] for xh in range(2)],
                axis=1,
            ).astype(jnp.bfloat16)
            for core in range(2)
        ]
        first_core = meta_ref[15] == 0
        keep_ref[z] = jnp.where(first_core, by_core[0], by_core[1])
        sent_ref[z] = jnp.where(first_core, by_core[1], by_core[0])
    put_sent = pltpu.make_async_copy(sent_ref, send_ref, done.at[2])
    put_sent.start()

    def read_home(which, head, first, count):
        start = pl.multiple_of(home_first + first, 128)
        return qkv_ref[pl.ds(start, count), columns(which, head)]

    def read_move(which, head, first, count):
        return move_ref[pl.ds(first, count), columns(which, head)]

    out_ref[HOME:, :] = jnp.zeros((GROUP - HOME, 3 * FEAT), jnp.bfloat16)
    backward_clip(
        read_home, HOME, home_prob_ref, 0, ga_ref, att_ref, out_ref, key_acc, value_acc
    )
    start = pltpu.make_async_copy(
        out_ref.at[:HOME_MIN, :], grads_ref.at[:HOME_MIN, :], done.at[0]
    )
    start.start()
    backward_clip(
        read_move, MOVE, move_prob_ref, home_len, ga_ref, att_ref, out_ref, key_acc, value_acc
    )
    end = pltpu.make_async_copy(
        out_ref.at[HOME_MIN:, :], grads_ref.at[HOME_MIN:, :], done.at[1]
    )
    end.start()
    start.wait()
    end.wait()
    put_sent.wait()


def backward(meta, qkv, moved, att, home_prob, move_prob, near, far, weight, last_blocks, part):
    return pl.pallas_call(
        backward_kernel,
        out_shape=(
            pltpu.HBM((GROUP, 3 * FEAT), jnp.bfloat16),
            pltpu.HBM((4, FEAT, D // 8), jnp.bfloat16),
            jax.ShapeDtypeStruct((4, FEAT, D // 8), jnp.bfloat16),
        ),
        in_specs=[SMEM] + [VMEM] * 12,
        out_specs=(HBM, HBM, VMEM),
        scratch_shapes=[
            pltpu.VMEM((GROUP, 3 * FEAT), jnp.bfloat16),
            pltpu.VMEM((GROUP, FEAT), jnp.bfloat16),
            pltpu.VMEM((HOME, FEAT), jnp.float32),
            pltpu.VMEM((HOME, FEAT), jnp.float32),
            pltpu.VMEM((4, FEAT, D // 8), jnp.bfloat16),
            pltpu.SemaphoreType.DMA((3,)),
        ],
        compiler_params=PARAMS,
        cost_estimate=pl.CostEstimate(
            flops=10_000_000_000, bytes_accessed=12_000_000, transcendentals=0
        ),
        name="backward",
    )(meta, qkv, moved, att, home_prob, move_prob, near, far, weight, *last_blocks, part)


def pick(x, index):
    return lax.dynamic_index_in_dim(x, index, 0, keepdims=False)


def both_cores_kernel(z_ref, keep_ref, got_ref, *outs):
    for distance, out in enumerate(outs):
        at = lax.rem(z_ref[0] + distance, 4)
        both = keep_ref[at].astype(jnp.float32) + got_ref[at].astype(jnp.float32)
        out[...] = both.astype(jnp.bfloat16)


def both_cores(z, keep, got):
    return pl.pallas_call(
        both_cores_kernel,
        out_shape=(jax.ShapeDtypeStruct((FEAT, D // 8), jnp.bfloat16),) * 4,
        in_specs=[SMEM, VMEM, VMEM],
        out_specs=(VMEM,) * 4,
        compiler_params=PARAMS,
        cost_estimate=pl.CostEstimate(flops=0, bytes_accessed=3_000_000, transcendentals=0),
        name="both_cores",
    )(z.reshape(1).astype(jnp.int32), keep, got)


def summed_over_groups(send, keep):
    group_id = lax.axis_index("dp")
    z, xh = group_id // 4, group_id // 2 % 2
    got = lax.ppermute(send, "dp", [(i, i ^ 1) for i in range(16)])
    mine, *rest = both_cores(z, keep, got)
    total = mine.astype(jnp.float32)
    for distance, sent in enumerate(rest, 1):
        total = total + shifted(sent, "dp", 4 * distance).astype(jnp.float32)
    low, high = total[:, : D // 16], total[:, D // 16 :]
    sent = jnp.where(xh == 0, high, low).astype(jnp.bfloat16)
    got = lax.ppermute(sent, "dp", [(i, i ^ 2) for i in range(16)])
    return jnp.where(xh == 0, low, high) + got.astype(jnp.float32)


def arriving(distance, outgoing, qkv, meta, weight, *blocks):
    moved = shifted(outgoing, "dp", distance)
    home_att, home_prob = forward_home(meta, qkv)
    near = grad_att(weight, blocks)
    return moved, home_att, home_prob, near


def local(query_rows, key_rows, value_rows, out_grad, out_weight, clip_len, clip_group, clip_start):
    groups = lax.axis_size("dp")
    group_id = lax.axis_index("dp")
    me = lax.axis_index("head")
    rotate_by = jnp.mod(clip_group[1] - clip_group[0], groups)
    source_group = jnp.mod(group_id - rotate_by, groups)
    half, third = ROWS // 2, ROWS // 3

    up, down = ((me + 6) % 8) * ROWS, ((me + 2) % 8) * ROWS
    far_a = ((me + 4) % 8) * ROWS
    far_b, far_c = (((me + 2) % 8) ^ 1) * ROWS, (((me + 6) % 8) ^ 1) * ROWS
    far_d = (((me + 4) % 8) ^ 1) * ROWS
    meta = jnp.stack(
        [
            clip_start[2 * group_id],
            clip_len[2 * group_id],
            clip_len[2 * source_group + 1],
            jnp.int32(0),
            me * ROWS,
            (me ^ 1) * ROWS,
            up,
            down,
            far_a,
            far_c,
            far_a + half,
            far_b + third,
            far_b,
            far_c + 2 * third,
            far_d,
            group_id % 2,
        ]
    ).astype(jnp.int32)

    dy_x = swapped(out_grad)
    dy_up = shifted(out_grad, "head", 2)
    dy_down = shifted(out_grad, "head", -2)

    packed = jnp.concatenate(
        [x.reshape(ROWS, 8, FEAT) for x in (query_rows, key_rows, value_rows)], axis=2
    )
    qkv = lax.all_to_all(packed, "head", split_axis=1, concat_axis=0, tiled=False)
    qkv = qkv.reshape(GROUP, 3 * FEAT)
    padded = jnp.concatenate([qkv, jnp.zeros((MOVE // 2, 3 * FEAT), jnp.bfloat16)], axis=0)
    outgoing = lax.dynamic_slice_in_dim(padded, clip_start[2 * group_id + 1], MOVE, 0)

    got_up = shifted(jnp.concatenate([dy_up[:half], dy_x[: 2 * third]]), "head", 2)
    got_down = shifted(jnp.concatenate([dy_down[half:], dy_x[third:]]), "head", -2)
    got_x = swapped(jnp.concatenate([dy_down[:third], dy_up[2 * third :]]))

    near_blocks = [out_grad, dy_x, dy_up, dy_down]
    moved, home_att, home_prob, near = lax.switch(
        rotate_by - 1,
        [functools.partial(arriving, d) for d in range(1, groups // 2 + 1)],
        outgoing, qkv, meta, out_weight, *near_blocks,
    )

    moved, got_up, got_down, got_x = lax.optimization_barrier((moved, got_up, got_down, got_x))
    last_blocks = [
        shifted(got_up[half : half + third], "head", 2),
        swapped(jnp.concatenate([got_up[third:half], got_down[: 2 * third - half]])),
        shifted(got_down[-third:], "head", -2),
    ]
    far_blocks = [got_up, got_down, got_x]
    att, move_prob, far, part = middle(
        meta, moved, home_att, out_weight, near_blocks, far_blocks, (ROWS,) * 4 + FAR_PIECES
    )
    grads, send, keep = backward(
        meta, qkv, moved, att, home_prob, move_prob, near, far, out_weight, last_blocks, part
    )
    grad_weight = summed_over_groups(send, keep) * ((GROUP * groups) ** (-0.5))
    outs = apart(
        lax.all_to_all(
            grads.reshape(8, ROWS, 3 * FEAT), "head", split_axis=0, concat_axis=0, tiled=True
        )
    )
    return (*outs, grad_weight)


def solution(mesh):
    rows = P(("dp", "head"), None)
    in_specs = (rows, rows, rows, rows, P("head", None), P(), P(), P())
    out_specs = (rows, rows, rows, P("head", "dp"))
    return jax.shard_map(local, mesh=mesh, in_specs=in_specs, out_specs=out_specs, check_vma=False)
```

```python
import functools

import jax
import jax.numpy as jnp
from jax import lax
from jax.experimental import pallas as pl
from jax.experimental.pallas import tpu as pltpu
from jax.sharding import PartitionSpec as P

D = 3072
HD = 128
FEAT = 256
ROWS = 192
GROUP = 1536
HOME = 1024
MOVE = 512
HOME_MIN = 768
MOVE_MIN = 256
FAR_PIECES = (96, 128, 96, 128, 64, 64)
QB = 256
BQ = 1024
SCALE = HD ** (-0.5)
EXP2_SCALE = SCALE * 1.4426950408889634
NEG_BIG = -1e30
NN = (((1,), (0,)), ((), ()))
NT = (((1,), (1,)), ((), ()))
VMEM = pl.BlockSpec(memory_space=pltpu.VMEM)
SMEM = pl.BlockSpec(memory_space=pltpu.SMEM)
HBM = pl.BlockSpec(memory_space=pltpu.HBM)
PARAMS = pltpu.CompilerParams(vmem_limit_bytes=32 * 1024 * 1024)


def dot(a, b, dims=NN):
    return lax.dot_general(a, b, dims, preferred_element_type=jnp.float32)


def flip(x):
    return x.astype(jnp.float32).T.astype(x.dtype)


def apart_kernel(packed_ref, *outs):
    for i, out in enumerate(outs):
        for j in range(4):
            out[:, j * FEAT : (j + 1) * FEAT] = packed_ref[j, :, i * FEAT : (i + 1) * FEAT]


def apart(packed):
    return pl.pallas_call(
        apart_kernel,
        grid=(2,),
        out_shape=(jax.ShapeDtypeStruct((ROWS, 8 * FEAT), jnp.bfloat16),) * 3,
        in_specs=[pl.BlockSpec((4, ROWS, 3 * FEAT), lambda i: (i, 0, 0))],
        out_specs=(pl.BlockSpec((ROWS, 4 * FEAT), lambda i: (0, i)),) * 3,
        compiler_params=PARAMS,
        name="apart",
    )(packed)


def shifted(x, axis, distance):
    n = lax.axis_size(axis)
    return lax.ppermute(x, axis, [((i - distance) % n, i) for i in range(n)])


def swapped(x):
    return lax.ppermute(x, "head", [(i, i ^ 1) for i in range(8)])


def columns(which, head):
    return pl.ds(pl.multiple_of(which * FEAT + head * HD, HD), HD)


def forward_clip(read, length, rows, sure, prob_ref, att_ref, att_first, step_rows):
    def one_head(head, _):
        k = read(1, head, 0, rows)
        v_t = flip(read(2, head, 0, rows))

        def block(step, _):
            first = pl.multiple_of(step * step_rows, step_rows)
            q = read(0, head, first, step_rows)
            scores = dot(k, q, NT)
            key = lax.broadcasted_iota(jnp.int32, (rows - sure, step_rows), 0) + sure
            scores = jnp.concatenate(
                [scores[:sure], jnp.where(key < length, scores[sure:], NEG_BIG)], axis=0
            )
            peak = jnp.max(scores, axis=0, keepdims=True)
            unnorm = jnp.exp2((scores - peak) * EXP2_SCALE)
            total = jnp.sum(unnorm, axis=0, keepdims=True)
            query = lax.broadcasted_iota(jnp.int32, (1, step_rows), 1) + first
            prob = (unnorm * jnp.where(query < length, 1.0 / total, 0.0)).astype(jnp.bfloat16)
            prob_ref[head, :, pl.ds(first, step_rows)] = prob
            att = dot(v_t, prob).T.astype(jnp.bfloat16)
            there = pl.ds(pl.multiple_of(att_first + first, 128), step_rows)
            att_ref[there, columns(0, head)] = att
            return 0

        return lax.fori_loop(0, rows // step_rows, block, 0)

    lax.fori_loop(0, 2, one_head, 0)


def forward_home_kernel(meta_ref, qkv_ref, att_ref, prob_ref):
    home_first, home_len = meta_ref[0], meta_ref[1]

    def read(which, head, first, count):
        start = pl.multiple_of(home_first + first, 128)
        return qkv_ref[pl.ds(start, count), columns(which, head)]

    forward_clip(read, home_len, HOME, HOME_MIN, prob_ref, att_ref, 0, QB)


def forward_home(meta, qkv):
    return pl.pallas_call(
        forward_home_kernel,
        out_shape=(
            jax.ShapeDtypeStruct((HOME, FEAT), jnp.bfloat16),
            jax.ShapeDtypeStruct((2, HOME, HOME), jnp.bfloat16),
        ),
        in_specs=[SMEM, VMEM],
        out_specs=(VMEM, VMEM),
        compiler_params=PARAMS,
        cost_estimate=pl.CostEstimate(
            flops=6_000_000_000, bytes_accessed=8_000_000, transcendentals=2_100_000
        ),
        name="forward_home",
    )(meta, qkv)


def grad_att_kernel(count, weight_ref, *refs):
    blocks = refs[:count]
    out_ref, acc = refs[-2:]
    step = pl.program_id(0)

    @pl.when(step == 0)
    def _():
        acc[...] = jnp.zeros_like(acc)

    dy = jnp.concatenate([block[...] for block in blocks], axis=0)
    acc[...] += dot(dy, weight_ref[...], NT)

    @pl.when(step == pl.num_programs(0) - 1)
    def _():
        out_ref[...] = acc[...].astype(jnp.bfloat16)


def grad_att(weight, blocks):
    count = len(blocks)
    total = sum(block.shape[0] for block in blocks)
    wide = D // 4
    return pl.pallas_call(
        functools.partial(grad_att_kernel, count),
        grid=(4,),
        out_shape=jax.ShapeDtypeStruct((total, FEAT), jnp.bfloat16),
        in_specs=[
            pl.BlockSpec((FEAT, wide), lambda j: (0, j)),
            *[pl.BlockSpec((block.shape[0], wide), lambda j: (0, j)) for block in blocks],
        ],
        out_specs=pl.BlockSpec((total, FEAT), lambda j: (0, 0)),
        scratch_shapes=[pltpu.VMEM((total, FEAT), jnp.float32)],
        compiler_params=PARAMS,
        cost_estimate=pl.CostEstimate(
            flops=total * 300_000, bytes_accessed=total * 650, transcendentals=0
        ),
        name="grad_att",
    )(weight, *blocks)


def middle_kernel(pieces, n_far, meta_ref, move_ref, home_att_ref, weight_ref, *refs):
    blocks = refs[:-6]
    att_ref, prob_ref, grad_att_ref, out_ref, att_t, acc = refs[-6:]
    step = pl.program_id(0)

    def read(which, head, first, count):
        return move_ref[pl.ds(first, count), columns(which, head)]

    @pl.when(step == 0)
    def _():
        att_ref[:HOME, :] = home_att_ref[...]
        att_ref[HOME:, :] = jnp.zeros((GROUP - HOME, FEAT), jnp.bfloat16)
        forward_clip(read, meta_ref[2], MOVE, MOVE_MIN, prob_ref, att_ref, meta_ref[1], MOVE)
        picked = [
            att_ref[pl.ds(pl.multiple_of(meta_ref[4 + i], 32), count), :]
            for i, count in enumerate(pieces)
        ]
        att_t[...] = flip(jnp.concatenate(picked, axis=0))
        acc[...] = jnp.zeros_like(acc)

    dy = [block[...] for block in blocks]
    acc[...] += dot(jnp.concatenate(dy[-n_far:], axis=0), weight_ref[...], NT)
    out_ref[0] = dot(att_t[...], jnp.concatenate(dy, axis=0))

    @pl.when(step == pl.num_programs(0) - 1)
    def _():
        grad_att_ref[...] = acc[...].astype(jnp.bfloat16)


def middle(meta, moved, home_att, weight, near, far, pieces):
    blocks = near + far
    total = sum(pieces)
    far_rows = sum(block.shape[0] for block in far)
    wide = D // 4
    return pl.pallas_call(
        functools.partial(middle_kernel, pieces, len(far)),
        grid=(4,),
        out_shape=(
            jax.ShapeDtypeStruct((GROUP, FEAT), jnp.bfloat16),
            jax.ShapeDtypeStruct((2, MOVE, MOVE), jnp.bfloat16),
            jax.ShapeDtypeStruct((far_rows, FEAT), jnp.bfloat16),
            jax.ShapeDtypeStruct((4, FEAT, wide), jnp.float32),
        ),
        in_specs=[
            SMEM,
            VMEM,
            VMEM,
            pl.BlockSpec((FEAT, wide), lambda j: (0, j)),
            *[pl.BlockSpec((block.shape[0], wide), lambda j: (0, j)) for block in blocks],
        ],
        out_specs=(
            VMEM,
            VMEM,
            pl.BlockSpec((far_rows, FEAT), lambda j: (0, 0)),
            pl.BlockSpec((1, FEAT, wide), lambda j: (j, 0, 0)),
        ),
        scratch_shapes=[
            pltpu.VMEM((FEAT, total), jnp.bfloat16),
            pltpu.VMEM((far_rows, FEAT), jnp.float32),
        ],
        compiler_params=PARAMS,
        cost_estimate=pl.CostEstimate(
            flops=total * 600_000, bytes_accessed=total * 1_000, transcendentals=0
        ),
        name="middle",
    )(meta, moved, home_att, weight, *blocks)


def backward_clip(read, rows, prob_ref, row_first, ga_ref, att_ref, out_ref, key_acc, value_acc):
    block_rows = min(rows, BQ)
    k_t = [flip(read(1, head, 0, rows)) for head in range(2)]
    key_acc[:rows, :] = jnp.zeros((rows, FEAT), jnp.float32)
    value_acc[:rows, :] = jnp.zeros((rows, FEAT), jnp.float32)

    def block(step, _):
        first = pl.multiple_of(step * block_rows, block_rows)
        there = pl.ds(pl.multiple_of(row_first + first, 128), block_rows)
        for head in range(2):
            side = slice(head * HD, (head + 1) * HD)
            q = read(0, head, first, block_rows)
            v = read(2, head, 0, rows)
            prob = prob_ref[head, :, pl.ds(first, block_rows)]
            grad_att = ga_ref[there, side]
            product = grad_att.astype(jnp.float32) * att_ref[there, side].astype(jnp.float32)
            row_dot = jnp.sum(product.T, axis=0, keepdims=True)
            grad_prob = dot(v, grad_att, NT)
            grad_score = (prob.astype(jnp.float32) * (grad_prob - row_dot)).astype(jnp.bfloat16)
            value_acc[:rows, side] += dot(prob, grad_att)
            key_acc[:rows, side] += dot(grad_score, q)
            grad_query = (dot(k_t[head], grad_score) * SCALE).T.astype(jnp.bfloat16)
            out_ref[there, side] = grad_query
        return 0

    lax.fori_loop(0, rows // block_rows, block, 0)
    whole = pl.ds(pl.multiple_of(row_first, 128), rows)
    out_ref[whole, FEAT : 2 * FEAT] = (key_acc[:rows, :] * SCALE).astype(jnp.bfloat16)
    out_ref[whole, 2 * FEAT :] = value_acc[:rows, :].astype(jnp.bfloat16)


def backward_kernel(
    meta_ref, qkv_ref, move_ref, att_ref, home_prob_ref, move_prob_ref,
    near_ref, far_ref, weight_ref, last_a, last_b, last_c, sum_ref,
    grads_ref, send_ref, keep_ref, out_ref, ga_ref, key_acc, value_acc, sent_ref, done,
):
    home_first, home_len = meta_ref[0], meta_ref[1]
    half = ROWS // 2
    for i in range(4):
        first = pl.multiple_of(meta_ref[4 + i], half)
        ga_ref[pl.ds(first, ROWS), :] = near_ref[i * ROWS : (i + 1) * ROWS, :]
    at = 0
    for i, count in enumerate(FAR_PIECES):
        first = pl.multiple_of(meta_ref[8 + i], 32)
        ga_ref[pl.ds(first, count), :] = far_ref[at : at + count, :]
        at += count
    dy = jnp.concatenate([last_a[...], last_b[...], last_c[...]], axis=0)
    last = dot(dy, weight_ref[...], NT).astype(jnp.bfloat16)
    last_rows = pl.ds(pl.multiple_of(meta_ref[14], half), ROWS)
    ga_ref[last_rows, :] = last

    att_t = flip(att_ref[last_rows, :])
    wide, cut = D // 4, D // 16
    for z in range(4):
        whole = sum_ref[z] + dot(att_t, dy[:, z * wide : (z + 1) * wide])
        by_core = [
            jnp.concatenate(
                [whole[:, (2 * xh + core) * cut : (2 * xh + core + 1) * cut] for xh in range(2)],
                axis=1,
            ).astype(jnp.bfloat16)
            for core in range(2)
        ]
        first_core = meta_ref[15] == 0
        keep_ref[z] = jnp.where(first_core, by_core[0], by_core[1])
        sent_ref[z] = jnp.where(first_core, by_core[1], by_core[0])
    put_sent = pltpu.make_async_copy(sent_ref, send_ref, done.at[2])
    put_sent.start()

    def read_home(which, head, first, count):
        start = pl.multiple_of(home_first + first, 128)
        return qkv_ref[pl.ds(start, count), columns(which, head)]

    def read_move(which, head, first, count):
        return move_ref[pl.ds(first, count), columns(which, head)]

    out_ref[HOME:, :] = jnp.zeros((GROUP - HOME, 3 * FEAT), jnp.bfloat16)
    backward_clip(
        read_home, HOME, home_prob_ref, 0, ga_ref, att_ref, out_ref, key_acc, value_acc
    )
    start = pltpu.make_async_copy(
        out_ref.at[:HOME_MIN, :], grads_ref.at[:HOME_MIN, :], done.at[0]
    )
    start.start()
    backward_clip(
        read_move, MOVE, move_prob_ref, home_len, ga_ref, att_ref, out_ref, key_acc, value_acc
    )
    end = pltpu.make_async_copy(
        out_ref.at[HOME_MIN:, :], grads_ref.at[HOME_MIN:, :], done.at[1]
    )
    end.start()
    start.wait()
    end.wait()
    put_sent.wait()


def backward(meta, qkv, moved, att, home_prob, move_prob, near, far, weight, last_blocks, part):
    return pl.pallas_call(
        backward_kernel,
        out_shape=(
            pltpu.HBM((GROUP, 3 * FEAT), jnp.bfloat16),
            pltpu.HBM((4, FEAT, D // 8), jnp.bfloat16),
            jax.ShapeDtypeStruct((4, FEAT, D // 8), jnp.bfloat16),
        ),
        in_specs=[SMEM] + [VMEM] * 12,
        out_specs=(HBM, HBM, VMEM),
        scratch_shapes=[
            pltpu.VMEM((GROUP, 3 * FEAT), jnp.bfloat16),
            pltpu.VMEM((GROUP, FEAT), jnp.bfloat16),
            pltpu.VMEM((HOME, FEAT), jnp.float32),
            pltpu.VMEM((HOME, FEAT), jnp.float32),
            pltpu.VMEM((4, FEAT, D // 8), jnp.bfloat16),
            pltpu.SemaphoreType.DMA((3,)),
        ],
        compiler_params=PARAMS,
        cost_estimate=pl.CostEstimate(
            flops=10_000_000_000, bytes_accessed=12_000_000, transcendentals=0
        ),
        name="backward",
    )(meta, qkv, moved, att, home_prob, move_prob, near, far, weight, *last_blocks, part)


def pick(x, index):
    return lax.dynamic_index_in_dim(x, index, 0, keepdims=False)


def both_cores_kernel(z_ref, keep_ref, got_ref, *outs):
    for distance, out in enumerate(outs):
        at = lax.rem(z_ref[0] + distance, 4)
        both = keep_ref[at].astype(jnp.float32) + got_ref[at].astype(jnp.float32)
        out[...] = both.T.astype(jnp.bfloat16)


def both_cores(z, keep, got):
    return pl.pallas_call(
        both_cores_kernel,
        out_shape=(jax.ShapeDtypeStruct((D // 8, FEAT), jnp.bfloat16),) * 4,
        in_specs=[SMEM, VMEM, VMEM],
        out_specs=(VMEM,) * 4,
        compiler_params=PARAMS,
        cost_estimate=pl.CostEstimate(flops=0, bytes_accessed=3_000_000, transcendentals=0),
        name="both_cores",
    )(z.reshape(1).astype(jnp.int32), keep, got)


def summed_over_groups(send, keep):
    group_id = lax.axis_index("dp")
    z, xh = group_id // 4, group_id // 2 % 2
    got = lax.ppermute(send, "dp", [(i, i ^ 1) for i in range(16)])
    mine, *rest = both_cores(z, keep, got)
    total = mine.astype(jnp.float32)
    for distance, sent in enumerate(rest, 1):
        total = total + shifted(sent, "dp", 4 * distance).astype(jnp.float32)
    low, high = total[: D // 16], total[D // 16 :]
    sent = jnp.where(xh == 0, high, low).astype(jnp.bfloat16)
    got = lax.ppermute(sent, "dp", [(i, i ^ 2) for i in range(16)])
    return (jnp.where(xh == 0, low, high) + got.astype(jnp.float32)).T


def arriving(distance, outgoing, qkv, meta, weight, *blocks):
    moved = shifted(outgoing, "dp", distance)
    home_att, home_prob = forward_home(meta, qkv)
    near = grad_att(weight, blocks)
    return moved, home_att, home_prob, near


def local(query_rows, key_rows, value_rows, out_grad, out_weight, clip_len, clip_group, clip_start):
    groups = lax.axis_size("dp")
    group_id = lax.axis_index("dp")
    me = lax.axis_index("head")
    rotate_by = jnp.mod(clip_group[1] - clip_group[0], groups)
    source_group = jnp.mod(group_id - rotate_by, groups)
    half, third = ROWS // 2, ROWS // 3

    up, down = ((me + 6) % 8) * ROWS, ((me + 2) % 8) * ROWS
    far_a = ((me + 4) % 8) * ROWS
    far_b, far_c = (((me + 2) % 8) ^ 1) * ROWS, (((me + 6) % 8) ^ 1) * ROWS
    far_d = (((me + 4) % 8) ^ 1) * ROWS
    meta = jnp.stack(
        [
            clip_start[2 * group_id],
            clip_len[2 * group_id],
            clip_len[2 * source_group + 1],
            jnp.int32(0),
            me * ROWS,
            (me ^ 1) * ROWS,
            up,
            down,
            far_a,
            far_c,
            far_a + half,
            far_b + third,
            far_b,
            far_c + 2 * third,
            far_d,
            group_id % 2,
        ]
    ).astype(jnp.int32)

    dy_x = swapped(out_grad)
    dy_up = shifted(out_grad, "head", 2)
    dy_down = shifted(out_grad, "head", -2)

    packed = jnp.concatenate(
        [x.reshape(ROWS, 8, FEAT) for x in (query_rows, key_rows, value_rows)], axis=2
    )
    qkv = lax.all_to_all(packed, "head", split_axis=1, concat_axis=0, tiled=False)
    qkv = qkv.reshape(GROUP, 3 * FEAT)
    padded = jnp.concatenate([qkv, jnp.zeros((MOVE // 2, 3 * FEAT), jnp.bfloat16)], axis=0)
    outgoing = lax.dynamic_slice_in_dim(padded, clip_start[2 * group_id + 1], MOVE, 0)

    got_up = shifted(jnp.concatenate([dy_up[:half], dy_x[: 2 * third]]), "head", 2)
    got_down = shifted(jnp.concatenate([dy_down[half:], dy_x[third:]]), "head", -2)
    got_x = swapped(jnp.concatenate([dy_down[:third], dy_up[2 * third :]]))

    near_blocks = [out_grad, dy_x, dy_up, dy_down]
    moved, home_att, home_prob, near = lax.switch(
        rotate_by - 1,
        [functools.partial(arriving, d) for d in range(1, groups // 2 + 1)],
        outgoing, qkv, meta, out_weight, *near_blocks,
    )

    moved, got_up, got_down, got_x = lax.optimization_barrier((moved, got_up, got_down, got_x))
    last_blocks = [
        shifted(got_up[half : half + third], "head", 2),
        swapped(jnp.concatenate([got_up[third:half], got_down[: 2 * third - half]])),
        shifted(got_down[-third:], "head", -2),
    ]
    far_blocks = [got_up, got_down, got_x]
    att, move_prob, far, part = middle(
        meta, moved, home_att, out_weight, near_blocks, far_blocks, (ROWS,) * 4 + FAR_PIECES
    )
    grads, send, keep = backward(
        meta, qkv, moved, att, home_prob, move_prob, near, far, out_weight, last_blocks, part
    )
    grad_weight = summed_over_groups(send, keep) * ((GROUP * groups) ** (-0.5))
    outs = apart(
        lax.all_to_all(
            grads.reshape(8, ROWS, 3 * FEAT), "head", split_axis=0, concat_axis=0, tiled=True
        )
    )
    return (*outs, grad_weight)


def solution(mesh):
    rows = P(("dp", "head"), None)
    in_specs = (rows, rows, rows, rows, P("head", None), P(), P(), P())
    out_specs = (rows, rows, rows, P("head", "dp"))
    return jax.shard_map(local, mesh=mesh, in_specs=in_specs, out_specs=out_specs, check_vma=False)
```

```python
import functools

import jax
import jax.numpy as jnp
from jax import lax
from jax.experimental import pallas as pl
from jax.experimental.pallas import tpu as pltpu
from jax.sharding import PartitionSpec as P

D = 3072
HD = 128
FEAT = 256
ROWS = 192
GROUP = 1536
HOME = 1024
MOVE = 512
HOME_MIN = 768
MOVE_MIN = 256
FAR_PIECES = (96, 128, 96, 128, 64, 64)
QB = 256
SCALE = HD ** (-0.5)
EXP2_SCALE = SCALE * 1.4426950408889634
NEG_BIG = -1e30
NN = (((1,), (0,)), ((), ()))
NT = (((1,), (1,)), ((), ()))
VMEM = pl.BlockSpec(memory_space=pltpu.VMEM)
SMEM = pl.BlockSpec(memory_space=pltpu.SMEM)
HBM = pl.BlockSpec(memory_space=pltpu.HBM)
PARAMS = pltpu.CompilerParams(vmem_limit_bytes=32 * 1024 * 1024)


def dot(a, b, dims=NN):
    return lax.dot_general(a, b, dims, preferred_element_type=jnp.float32)


def flip(x):
    return x.T


def apart_kernel(packed_ref, *outs):
    for i, out in enumerate(outs):
        for j in range(4):
            out[:, j * FEAT : (j + 1) * FEAT] = packed_ref[j, :, i * FEAT : (i + 1) * FEAT]


def apart(packed):
    return pl.pallas_call(
        apart_kernel,
        grid=(2,),
        out_shape=(jax.ShapeDtypeStruct((ROWS, 8 * FEAT), jnp.bfloat16),) * 3,
        in_specs=[pl.BlockSpec((4, ROWS, 3 * FEAT), lambda i: (i, 0, 0))],
        out_specs=(pl.BlockSpec((ROWS, 4 * FEAT), lambda i: (0, i)),) * 3,
        compiler_params=PARAMS,
        name="apart",
    )(packed)


def shifted(x, axis, distance):
    n = lax.axis_size(axis)
    return lax.ppermute(x, axis, [((i - distance) % n, i) for i in range(n)])


def swapped(x):
    return lax.ppermute(x, "head", [(i, i ^ 1) for i in range(8)])


def columns(which, head):
    return pl.ds(pl.multiple_of(which * FEAT + head * HD, HD), HD)


def forward_clip(read, length, rows, sure, prob_ref, att_ref, att_first, step_rows):
    def one_head(head, _):
        k = read(1, head, 0, rows)
        v_t = flip(read(2, head, 0, rows))

        def block(step, _):
            first = pl.multiple_of(step * step_rows, step_rows)
            q = read(0, head, first, step_rows)
            scores = dot(k, q, NT)
            key = lax.broadcasted_iota(jnp.int32, (rows - sure, step_rows), 0) + sure
            scores = jnp.concatenate(
                [scores[:sure], jnp.where(key < length, scores[sure:], NEG_BIG)], axis=0
            )
            peak = jnp.max(scores, axis=0, keepdims=True)
            unnorm = jnp.exp2((scores - peak) * EXP2_SCALE)
            total = jnp.sum(unnorm, axis=0, keepdims=True)
            query = lax.broadcasted_iota(jnp.int32, (1, step_rows), 1) + first
            prob = (unnorm * jnp.where(query < length, 1.0 / total, 0.0)).astype(jnp.bfloat16)
            prob_ref[head, :, pl.ds(first, step_rows)] = prob
            att = dot(v_t, prob).T.astype(jnp.bfloat16)
            there = pl.ds(pl.multiple_of(att_first + first, 128), step_rows)
            att_ref[there, columns(0, head)] = att
            return 0

        return lax.fori_loop(0, rows // step_rows, block, 0)

    lax.fori_loop(0, 2, one_head, 0)


def forward_home_kernel(meta_ref, qkv_ref, att_ref, prob_ref):
    home_first, home_len = meta_ref[0], meta_ref[1]

    def read(which, head, first, count):
        start = pl.multiple_of(home_first + first, 128)
        return qkv_ref[pl.ds(start, count), columns(which, head)]

    forward_clip(read, home_len, HOME, HOME_MIN, prob_ref, att_ref, 0, QB)


def forward_home(meta, qkv):
    return pl.pallas_call(
        forward_home_kernel,
        out_shape=(
            jax.ShapeDtypeStruct((HOME, FEAT), jnp.bfloat16),
            jax.ShapeDtypeStruct((2, HOME, HOME), jnp.bfloat16),
        ),
        in_specs=[SMEM, VMEM],
        out_specs=(VMEM, VMEM),
        compiler_params=PARAMS,
        cost_estimate=pl.CostEstimate(
            flops=6_000_000_000, bytes_accessed=8_000_000, transcendentals=2_100_000
        ),
        name="forward_home",
    )(meta, qkv)


def grad_att_kernel(count, weight_ref, *refs):
    blocks = refs[:count]
    out_ref, acc = refs[-2:]
    step = pl.program_id(0)

    @pl.when(step == 0)
    def _():
        acc[...] = jnp.zeros_like(acc)

    dy = jnp.concatenate([block[...] for block in blocks], axis=0)
    acc[...] += dot(dy, weight_ref[...], NT)

    @pl.when(step == pl.num_programs(0) - 1)
    def _():
        out_ref[...] = acc[...].astype(jnp.bfloat16)


def grad_att(weight, blocks):
    count = len(blocks)
    total = sum(block.shape[0] for block in blocks)
    wide = D // 4
    return pl.pallas_call(
        functools.partial(grad_att_kernel, count),
        grid=(4,),
        out_shape=jax.ShapeDtypeStruct((total, FEAT), jnp.bfloat16),
        in_specs=[
            pl.BlockSpec((FEAT, wide), lambda j: (0, j)),
            *[pl.BlockSpec((block.shape[0], wide), lambda j: (0, j)) for block in blocks],
        ],
        out_specs=pl.BlockSpec((total, FEAT), lambda j: (0, 0)),
        scratch_shapes=[pltpu.VMEM((total, FEAT), jnp.float32)],
        compiler_params=PARAMS,
        cost_estimate=pl.CostEstimate(
            flops=total * 300_000, bytes_accessed=total * 650, transcendentals=0
        ),
        name="grad_att",
    )(weight, *blocks)


def middle_kernel(pieces, n_far, meta_ref, move_ref, home_att_ref, weight_ref, *refs):
    blocks = refs[:-6]
    att_ref, prob_ref, grad_att_ref, out_ref, att_t, acc = refs[-6:]
    step = pl.program_id(0)

    def read(which, head, first, count):
        return move_ref[pl.ds(first, count), columns(which, head)]

    @pl.when(step == 0)
    def _():
        att_ref[:HOME, :] = home_att_ref[...]
        att_ref[HOME:, :] = jnp.zeros((GROUP - HOME, FEAT), jnp.bfloat16)
        forward_clip(read, meta_ref[2], MOVE, MOVE_MIN, prob_ref, att_ref, meta_ref[1], MOVE)
        picked = [
            att_ref[pl.ds(pl.multiple_of(meta_ref[4 + i], 32), count), :]
            for i, count in enumerate(pieces)
        ]
        att_t[...] = flip(jnp.concatenate(picked, axis=0))
        acc[...] = jnp.zeros_like(acc)

    dy = [block[...] for block in blocks]
    acc[...] += dot(jnp.concatenate(dy[-n_far:], axis=0), weight_ref[...], NT)
    out_ref[0] = dot(att_t[...], jnp.concatenate(dy, axis=0))

    @pl.when(step == pl.num_programs(0) - 1)
    def _():
        grad_att_ref[...] = acc[...].astype(jnp.bfloat16)


def middle(meta, moved, home_att, weight, near, far, pieces):
    blocks = near + far
    total = sum(pieces)
    far_rows = sum(block.shape[0] for block in far)
    wide = D // 4
    return pl.pallas_call(
        functools.partial(middle_kernel, pieces, len(far)),
        grid=(4,),
        out_shape=(
            jax.ShapeDtypeStruct((GROUP, FEAT), jnp.bfloat16),
            jax.ShapeDtypeStruct((2, MOVE, MOVE), jnp.bfloat16),
            jax.ShapeDtypeStruct((far_rows, FEAT), jnp.bfloat16),
            jax.ShapeDtypeStruct((4, FEAT, wide), jnp.float32),
        ),
        in_specs=[
            SMEM,
            VMEM,
            VMEM,
            pl.BlockSpec((FEAT, wide), lambda j: (0, j)),
            *[pl.BlockSpec((block.shape[0], wide), lambda j: (0, j)) for block in blocks],
        ],
        out_specs=(
            VMEM,
            VMEM,
            pl.BlockSpec((far_rows, FEAT), lambda j: (0, 0)),
            pl.BlockSpec((1, FEAT, wide), lambda j: (j, 0, 0)),
        ),
        scratch_shapes=[
            pltpu.VMEM((FEAT, total), jnp.bfloat16),
            pltpu.VMEM((far_rows, FEAT), jnp.float32),
        ],
        compiler_params=PARAMS,
        cost_estimate=pl.CostEstimate(
            flops=total * 600_000, bytes_accessed=total * 1_000, transcendentals=0
        ),
        name="middle",
    )(meta, moved, home_att, weight, *blocks)


def backward_clip(read, rows, prob_ref, row_first, ga_ref, att_ref, out_ref):
    there = pl.ds(pl.multiple_of(row_first, 128), rows)
    for head in range(2):
        side = slice(head * HD, (head + 1) * HD)
        k_t = flip(read(1, head, 0, rows))
        prob = prob_ref[head]
        grad_att = ga_ref[there, side]
        product = grad_att.astype(jnp.float32) * att_ref[there, side].astype(jnp.float32)
        row_dot = jnp.sum(product.T, axis=0, keepdims=True)
        grad_prob = dot(read(2, head, 0, rows), grad_att, NT)
        grad_score = (prob.astype(jnp.float32) * (grad_prob - row_dot)).astype(jnp.bfloat16)
        grad_value = dot(prob, grad_att)
        grad_key = dot(grad_score, read(0, head, 0, rows)) * SCALE
        grad_query = (dot(k_t, grad_score) * SCALE).T
        out_ref[there, columns(0, head)] = grad_query.astype(jnp.bfloat16)
        out_ref[there, columns(1, head)] = grad_key.astype(jnp.bfloat16)
        out_ref[there, columns(2, head)] = grad_value.astype(jnp.bfloat16)


def backward_kernel(
    meta_ref, qkv_ref, move_ref, att_ref, home_prob_ref, move_prob_ref,
    near_ref, far_ref, weight_ref, last_a, last_b, last_c, sum_ref,
    grads_ref, send_ref, keep_ref, out_ref, ga_ref, sent_ref, done,
):
    home_first, home_len = meta_ref[0], meta_ref[1]
    half = ROWS // 2
    for i in range(4):
        first = pl.multiple_of(meta_ref[4 + i], half)
        ga_ref[pl.ds(first, ROWS), :] = near_ref[i * ROWS : (i + 1) * ROWS, :]
    at = 0
    for i, count in enumerate(FAR_PIECES):
        first = pl.multiple_of(meta_ref[8 + i], 32)
        ga_ref[pl.ds(first, count), :] = far_ref[at : at + count, :]
        at += count
    dy = jnp.concatenate([last_a[...], last_b[...], last_c[...]], axis=0)
    last = dot(dy, weight_ref[...], NT).astype(jnp.bfloat16)
    last_rows = pl.ds(pl.multiple_of(meta_ref[14], half), ROWS)
    ga_ref[last_rows, :] = last

    att_t = flip(att_ref[last_rows, :])
    wide, cut = D // 4, D // 16
    for z in range(4):
        whole = sum_ref[z] + dot(att_t, dy[:, z * wide : (z + 1) * wide])
        by_core = [
            jnp.concatenate(
                [whole[:, (2 * xh + core) * cut : (2 * xh + core + 1) * cut] for xh in range(2)],
                axis=1,
            ).astype(jnp.bfloat16)
            for core in range(2)
        ]
        first_core = meta_ref[15] == 0
        keep_ref[z] = jnp.where(first_core, by_core[0], by_core[1])
        sent_ref[z] = jnp.where(first_core, by_core[1], by_core[0])
    put_sent = pltpu.make_async_copy(sent_ref, send_ref, done.at[2])
    put_sent.start()

    def read_home(which, head, first, count):
        start = pl.multiple_of(home_first + first, 128)
        return qkv_ref[pl.ds(start, count), columns(which, head)]

    def read_move(which, head, first, count):
        return move_ref[pl.ds(first, count), columns(which, head)]

    out_ref[HOME:, :] = jnp.zeros((GROUP - HOME, 3 * FEAT), jnp.bfloat16)
    backward_clip(
        read_home, HOME, home_prob_ref, 0, ga_ref, att_ref, out_ref
    )
    start = pltpu.make_async_copy(
        out_ref.at[:HOME_MIN, :], grads_ref.at[:HOME_MIN, :], done.at[0]
    )
    start.start()
    backward_clip(
        read_move, MOVE, move_prob_ref, home_len, ga_ref, att_ref, out_ref
    )
    end = pltpu.make_async_copy(
        out_ref.at[HOME_MIN:, :], grads_ref.at[HOME_MIN:, :], done.at[1]
    )
    end.start()
    start.wait()
    end.wait()
    put_sent.wait()


def backward(meta, qkv, moved, att, home_prob, move_prob, near, far, weight, last_blocks, part):
    return pl.pallas_call(
        backward_kernel,
        out_shape=(
            pltpu.HBM((GROUP, 3 * FEAT), jnp.bfloat16),
            pltpu.HBM((4, FEAT, D // 8), jnp.bfloat16),
            jax.ShapeDtypeStruct((4, FEAT, D // 8), jnp.bfloat16),
        ),
        in_specs=[SMEM] + [VMEM] * 12,
        out_specs=(HBM, HBM, VMEM),
        scratch_shapes=[
            pltpu.VMEM((GROUP, 3 * FEAT), jnp.bfloat16),
            pltpu.VMEM((GROUP, FEAT), jnp.bfloat16),
            pltpu.VMEM((4, FEAT, D // 8), jnp.bfloat16),
            pltpu.SemaphoreType.DMA((3,)),
        ],
        compiler_params=PARAMS,
        cost_estimate=pl.CostEstimate(
            flops=10_000_000_000, bytes_accessed=12_000_000, transcendentals=0
        ),
        name="backward",
    )(meta, qkv, moved, att, home_prob, move_prob, near, far, weight, *last_blocks, part)


def pick(x, index):
    return lax.dynamic_index_in_dim(x, index, 0, keepdims=False)


def both_cores_kernel(z_ref, keep_ref, got_ref, *outs):
    for distance, out in enumerate(outs):
        at = lax.rem(z_ref[0] + distance, 4)
        both = keep_ref[at].astype(jnp.float32) + got_ref[at].astype(jnp.float32)
        out[...] = both.T.astype(jnp.bfloat16)


def both_cores(z, keep, got):
    return pl.pallas_call(
        both_cores_kernel,
        out_shape=(jax.ShapeDtypeStruct((D // 8, FEAT), jnp.bfloat16),) * 4,
        in_specs=[SMEM, VMEM, VMEM],
        out_specs=(VMEM,) * 4,
        compiler_params=PARAMS,
        cost_estimate=pl.CostEstimate(flops=0, bytes_accessed=3_000_000, transcendentals=0),
        name="both_cores",
    )(z.reshape(1).astype(jnp.int32), keep, got)


def summed_over_groups(send, keep):
    group_id = lax.axis_index("dp")
    z, xh = group_id // 4, group_id // 2 % 2
    got = lax.ppermute(send, "dp", [(i, i ^ 1) for i in range(16)])
    mine, *rest = both_cores(z, keep, got)
    total = mine.astype(jnp.float32)
    for distance, sent in enumerate(rest, 1):
        total = total + shifted(sent, "dp", 4 * distance).astype(jnp.float32)
    low, high = total[: D // 16], total[D // 16 :]
    sent = jnp.where(xh == 0, high, low).astype(jnp.bfloat16)
    got = lax.ppermute(sent, "dp", [(i, i ^ 2) for i in range(16)])
    return (jnp.where(xh == 0, low, high) + got.astype(jnp.float32)).T


def arriving(distance, outgoing, qkv, meta, weight, *blocks):
    moved = shifted(outgoing, "dp", distance)
    home_att, home_prob = forward_home(meta, qkv)
    near = grad_att(weight, blocks)
    return moved, home_att, home_prob, near


def local(query_rows, key_rows, value_rows, out_grad, out_weight, clip_len, clip_group, clip_start):
    groups = lax.axis_size("dp")
    group_id = lax.axis_index("dp")
    me = lax.axis_index("head")
    rotate_by = jnp.mod(clip_group[1] - clip_group[0], groups)
    source_group = jnp.mod(group_id - rotate_by, groups)
    half, third = ROWS // 2, ROWS // 3

    up, down = ((me + 6) % 8) * ROWS, ((me + 2) % 8) * ROWS
    far_a = ((me + 4) % 8) * ROWS
    far_b, far_c = (((me + 2) % 8) ^ 1) * ROWS, (((me + 6) % 8) ^ 1) * ROWS
    far_d = (((me + 4) % 8) ^ 1) * ROWS
    meta = jnp.stack(
        [
            clip_start[2 * group_id],
            clip_len[2 * group_id],
            clip_len[2 * source_group + 1],
            jnp.int32(0),
            me * ROWS,
            up,
            down,
            (me ^ 1) * ROWS,
            far_a,
            far_c,
            far_a + half,
            far_b + third,
            far_b,
            far_c + 2 * third,
            far_d,
            group_id % 2,
        ]
    ).astype(jnp.int32)

    dy_up = shifted(out_grad, "head", 2)
    dy_down = shifted(out_grad, "head", -2)
    dy_x = swapped(out_grad)

    packed = jnp.concatenate(
        [x.reshape(ROWS, 8, FEAT) for x in (query_rows, key_rows, value_rows)], axis=2
    )
    qkv = lax.all_to_all(packed, "head", split_axis=1, concat_axis=0, tiled=False)
    qkv = qkv.reshape(GROUP, 3 * FEAT)
    padded = jnp.concatenate([qkv, jnp.zeros((MOVE // 2, 3 * FEAT), jnp.bfloat16)], axis=0)
    outgoing = lax.dynamic_slice_in_dim(padded, clip_start[2 * group_id + 1], MOVE, 0)

    got_up = shifted(jnp.concatenate([dy_up[:half], dy_x[: 2 * third]]), "head", 2)
    got_down = shifted(jnp.concatenate([dy_down[half:], dy_x[third:]]), "head", -2)
    got_x = swapped(jnp.concatenate([dy_down[:third], dy_up[2 * third :]]))

    near_blocks = [out_grad, dy_up, dy_down, dy_x]
    moved, home_att, home_prob, near = lax.switch(
        rotate_by - 1,
        [functools.partial(arriving, d) for d in range(1, groups // 2 + 1)],
        outgoing, qkv, meta, out_weight, *near_blocks,
    )

    moved, got_up, got_down, got_x = lax.optimization_barrier((moved, got_up, got_down, got_x))
    last_blocks = [
        shifted(got_up[half : half + third], "head", 2),
        swapped(jnp.concatenate([got_up[third:half], got_down[: 2 * third - half]])),
        shifted(got_down[-third:], "head", -2),
    ]
    far_blocks = [got_up, got_down, got_x]
    att, move_prob, far, part = middle(
        meta, moved, home_att, out_weight, near_blocks, far_blocks, (ROWS,) * 4 + FAR_PIECES
    )
    grads, send, keep = backward(
        meta, qkv, moved, att, home_prob, move_prob, near, far, out_weight, last_blocks, part
    )
    grad_weight = summed_over_groups(send, keep) * ((GROUP * groups) ** (-0.5))
    outs = apart(
        lax.all_to_all(
            grads.reshape(8, ROWS, 3 * FEAT), "head", split_axis=0, concat_axis=0, tiled=True
        )
    )
    return (*outs, grad_weight)


def solution(mesh):
    rows = P(("dp", "head"), None)
    in_specs = (rows, rows, rows, rows, P("head", None), P(), P(), P())
    out_specs = (rows, rows, rows, P("head", "dp"))
    return jax.shard_map(local, mesh=mesh, in_specs=in_specs, out_specs=out_specs, check_vma=False)
```
